32 devices in a mesh: row: 4 (over z), rep: 8 (over y, x, core).
Axes of the slice: x: 2, y: 2, z: 4, core: 2. Of those that a mesh axis runs over, the one named last changes fastest.
Arguments:
- features: bfloat16 [8192, 256], P('row'), may hold values from 0 to 2
- self_weight: bfloat16 [256, 256], replicated, may hold values from -0.375 to 0.375
- neigh_weight: bfloat16 [256, 256], replicated, may hold values from -0.375 to 0.375
- out_bias: float32 [256], replicated, may hold values from -4 to 4
- tile_masks: int32 [8192, 32, 128], P('row', 'rep'), may hold values 0 or 1
- tile_live: int32 [64, 32], P('row', 'rep'), may hold values from 0 to 1, as said below
- tile_columns: int32 [64, 32], P('row', 'rep'), may hold values from 0 to 1
- node_degree: int32 [8192], P(('row', 'rep')), may hold values from 32 to 127
- cotangent: bfloat16 [8192, 256], P(('row', 'rep')), may hold values from -6 to 6
Outputs:
- hidden_out: bfloat16 [8192, 256], P(('row', 'rep'))
- grad_features: bfloat16 [8192, 256], P(('row', 'rep'))
- grad_self: float32 [256, 256], replicated
- grad_neigh: float32 [256, 256], replicated
- grad_bias: float32 [256], replicated
The draws below stay inside these ranges and needn't reach their ends.
Inputs may be any that keep to these rules, and one draw needn't show every extreme that they name: `tile_masks`: an edge bit; bits of slots without a tile are not read. `tile_live`: 1 where the slot holds a tile. `tile_columns`: the covered block among the 2 blocks of that column set and panel.
All inputs are finite; a program needn't handle non-finite values. No bound on the sum of `tile_masks` on one device may be relied on, other than what follows from the above.
Results may differ from the reference program's by a relative error of at most 0.0053.
Values may be sent and summed in bfloat16 or wider, within the bound.
No kernel may reach another device: no remote copies, remote signals or barrier semaphores. Data moves between devices by JAX's collectives and lax.ppermute only.
A program may use at most 128 MiB of HBM per device.

```python
import math
import jax
import jax.numpy as jnp
from jax import lax

F = 256
TILE = 128
RBD = 2
PB = 16
PANEL = 2048
NODES = 8192
BLOCKS = 64
N_ROW = 4
N_REP = 8


def draw_tile_live(key, part):
    heavy_key, slot_key = jax.random.split(key)
    heavy = jax.random.randint(heavy_key, (N_ROW, 1, N_REP, 1), 0, 8) == 0
    rolls = jax.random.randint(slot_key, (N_ROW, PB, N_REP, N_ROW), 0, 20)
    limit = jnp.where(heavy, 18, 6)
    present = jnp.where(rolls < limit, 1, 0).astype(jnp.int32)
    return present.reshape(BLOCKS, N_REP * N_ROW)


def plant(values, key, low, high):
    extent = values.shape
    index_at = [jax.random.randint(jax.random.fold_in(key, axis), (), 0, extent[axis]) for axis in range(len(extent))]
    values = values.at[tuple(index_at)].set(low)
    longest = extent.index(max(extent))
    index_at[longest] = (index_at[longest] + 1) % extent[longest]
    return values.at[tuple(index_at)].set(high)


def block_scale(own_key, extent, cuts, smallest, high):
    gain, own = 1.0, jax.random.fold_in(own_key, 6)
    for dim, blocks in cuts:
        draws = jnp.exp(jax.random.uniform(jax.random.fold_in(own, dim), (blocks,), jnp.float32, smallest / len(cuts), high / len(cuts)))
        gain = gain * jnp.repeat(draws, extent[dim] // blocks).reshape([-1 if axis == dim else 1 for axis in range(len(extent))])
    return gain


def scatter_about(rng, extent, scale, bound, pieces=(), kind=jnp.bfloat16):
    factor_of = block_scale(rng, extent, pieces, -0.22, 0.18) if pieces else 1.0
    entries = jax.random.normal(rng, extent, jnp.float32) * scale * factor_of
    return jnp.minimum(jnp.maximum(entries, -bound), bound).astype(kind)


def setup_inputs(seed: int = 0) -> dict:
    streams_of = jax.random.split(jax.random.key(seed), 10)
    features = jnp.clip(2.0 * jax.random.uniform(streams_of[0], (NODES, F), jnp.float32) ** block_scale(streams_of[0], (NODES, F), ((0, 4),), -0.2, 0.2), 0.0, 2.0).astype(jnp.bfloat16)
    self_weight = scatter_about(streams_of[1], (F, F), F ** -0.5, 0.375)
    neigh_weight = scatter_about(streams_of[2], (F, F), F ** -0.5, 0.375)
    out_bias = scatter_about(streams_of[3], (F,), 1.0, 4.0, (), jnp.float32)
    tile_masks = plant((jax.random.randint(streams_of[4], (NODES, N_REP * N_ROW, TILE), 0, 32) < 1).astype(jnp.int32), jax.random.fold_in(streams_of[4], 1), 0, 1)
    tile_live = draw_tile_live(jax.random.fold_in(streams_of[9], 71), 0)
    tile_columns = plant(jax.random.randint(streams_of[6], (BLOCKS, N_REP * N_ROW), 0, RBD), jax.random.fold_in(streams_of[6], 1), 0, RBD - 1).astype(jnp.int32)
    node_degree = plant(jax.random.randint(streams_of[7], (NODES,), N_REP * N_ROW * TILE // 128, N_REP * N_ROW * TILE // 32), jax.random.fold_in(streams_of[7], 1), N_REP * N_ROW * TILE // 128, (N_REP * N_ROW * TILE // 32) - 1).astype(jnp.int32)
    cotangent = scatter_about(streams_of[8], (NODES, F), 1.0, 6.0, ((0, 32),))
    return dict(features=features, self_weight=self_weight, neigh_weight=neigh_weight, out_bias=out_bias, tile_masks=tile_masks, tile_live=tile_live, tile_columns=tile_columns, node_degree=node_degree, cotangent=cotangent)


def activation(values):
    return jax.nn.gelu(values, approximate=True)

def reference(features, self_weight, neigh_weight, out_bias, tile_masks, tile_live, tile_columns, node_degree, cotangent):
    highest = lax.Precision.HIGHEST
    column_sets = jnp.moveaxis(features.reshape(N_ROW, N_REP, RBD, TILE, F), 1, 0)
    masks = tile_masks.reshape(N_ROW, PB, TILE, N_REP, N_ROW, TILE)
    present = tile_live.reshape(N_ROW, PB, N_REP, N_ROW)
    chosen = tile_columns.reshape(N_ROW, PB, N_REP, N_ROW)
    degree = node_degree.reshape(N_ROW, PANEL, 1).astype(jnp.float32)
    panels = features.reshape(N_ROW, PANEL, F)
    cot_panels = cotangent.reshape(N_ROW, PANEL, F)
    scale = 1.0 / math.sqrt(NODES)
    panel_ids = jnp.arange(N_ROW).astype(jnp.int32)
    block_ids = jnp.arange(RBD).astype(jnp.int32)
    contract = (((0,), (0,)), ((), ()))
    outputs = []
    direct_rows = []
    grad_self = jnp.zeros((F, F), jnp.float32)
    grad_neigh = jnp.zeros((F, F), jnp.float32)
    grad_bias = jnp.zeros((F,), jnp.float32)
    transposed = jnp.zeros((N_ROW, N_REP, RBD, TILE, F), jnp.float32)
    for owner in range(N_ROW):
        set_masks = jnp.moveaxis(masks[owner], 2, 0)
        set_present = jnp.moveaxis(present[owner], 1, 0)
        set_chosen = jnp.moveaxis(chosen[owner], 1, 0)

        def forward_set(carry, inputs):
            mask_set, live_set, chosen_set, feature_set = inputs
            weights = mask_set.astype(jnp.float32) * live_set.astype(jnp.float32)[:, None, :, None]
            picked = feature_set[panel_ids[None, :], chosen_set].astype(jnp.float32)
            return (carry + jnp.einsum('pisj,psjf->pif', weights, picked, precision=highest), None)
        agg_sum, _ = lax.scan(forward_set, jnp.zeros((PB, TILE, F), jnp.float32), (set_masks, set_present, set_chosen, column_sets))
        agg_sum = agg_sum.reshape(PANEL, F)
        mean = (agg_sum / degree[owner]).astype(jnp.bfloat16)
        own = panels[owner]
        pre = jnp.dot(own, self_weight, preferred_element_type=jnp.float32) + jnp.dot(mean, neigh_weight, preferred_element_type=jnp.float32) + out_bias.astype(jnp.float32)
        result, pull = jax.vjp(activation, pre)
        outputs.append(result.astype(jnp.bfloat16))
        dpre = pull(cot_panels[owner].astype(jnp.float32))[0]
        dpre_b = dpre.astype(jnp.bfloat16)
        grad_self = grad_self + lax.dot_general(own, dpre_b, contract, preferred_element_type=jnp.float32)
        grad_neigh = grad_neigh + lax.dot_general(mean, dpre_b, contract, preferred_element_type=jnp.float32)
        grad_bias = grad_bias + lax.optimization_barrier(jnp.sum(dpre, axis=0))
        message = (jnp.dot(dpre_b, neigh_weight.T, preferred_element_type=jnp.float32) / degree[owner]).astype(jnp.bfloat16)
        direct_rows.append(jnp.dot(dpre_b, self_weight.T, preferred_element_type=jnp.float32))
        message_blocks = message.reshape(PB, TILE, F).astype(jnp.float32)

        def backward_set(inputs):
            mask_set, live_set, chosen_set = inputs
            weights = mask_set.astype(jnp.float32) * live_set.astype(jnp.float32)[:, None, :, None]
            per_tile = jnp.einsum('pisj,pif->psjf', weights, message_blocks, precision=highest)
            onehot = (chosen_set[:, :, None] == block_ids[None, None, :]).astype(jnp.float32)
            return jnp.einsum('psb,psjf->sbjf', onehot, per_tile, precision=highest)
        spread = lax.map(backward_set, (set_masks, set_present, set_chosen))
        transposed = transposed + jnp.moveaxis(spread, 0, 1)
    hidden_out = jnp.stack(outputs).reshape(NODES, F)
    direct = jnp.stack(direct_rows)
    grad_features = (direct + transposed.reshape(N_ROW, PANEL, F)).astype(jnp.bfloat16).reshape(NODES, F)
    return (hidden_out, grad_features, grad_self * scale, grad_neigh * scale, grad_bias * scale)
```

```python
import functools
import math

import jax
import jax.numpy as jnp
from jax import lax
from jax.experimental import pallas as pl
from jax.experimental.pallas import tpu as pltpu
from jax.sharding import PartitionSpec as P

BF16 = jnp.bfloat16
F32 = jnp.float32
BIAS_ROWS = 16
VMEM_LIMIT = 40 * 1024 * 1024
CONTRACT_FIRST = (((0,), (0,)), ((), ()))
CONTRACT_SECOND = (((1,), (1,)), ((), ()))
GELU_A = math.sqrt(2.0 / math.pi)
GELU_B = 0.044715


def dot(a, b, dims=(((1,), (0,)), ((), ()))):
    return lax.dot_general(a, b, dims, preferred_element_type=F32)


def params():
    return pltpu.CompilerParams(vmem_limit_bytes=VMEM_LIMIT)


def cost(flops, bytes_accessed):
    return pl.CostEstimate(flops=flops, bytes_accessed=bytes_accessed, transcendentals=0)


def whole(n):
    return [pl.BlockSpec(memory_space=pltpu.VMEM)] * n


def xor_permute(value, axis, k):
    return lax.ppermute(value, axis, [(i, i ^ k) for i in range(lax.axis_size(axis))])


def strip_kernel(panels, blocks, tile, live_ref, cols_ref, mask_ref, dense_ref, flip_ref):
    step = pl.program_id(0)
    for j in range(blocks):
        i = step * blocks + j
        for s in range(panels):
            bits = mask_ref[pl.ds(j * tile * panels + s, tile, stride=panels), :].astype(F32)
            turned = bits.T
            live = live_ref[s, i] != 0
            col = cols_ref[s, i]
            for b in range(blocks):
                keep = jnp.where(live & (col == b), 1.0, 0.0).astype(F32)
                at = (s * blocks + b) * tile
                dense_ref[j * tile : (j + 1) * tile, at : at + tile] = (bits * keep).astype(BF16)
                flip_ref[0, at : at + tile, j * tile : (j + 1) * tile] = (turned * keep).astype(BF16)


def build_strip(masks, live, cols, panels, blocks, tile, steps):
    share = blocks * tile
    width = panels * share
    return pl.pallas_call(
        functools.partial(strip_kernel, panels, blocks, tile),
        grid=(steps,),
        in_specs=[
            pl.BlockSpec(memory_space=pltpu.SMEM),
            pl.BlockSpec(memory_space=pltpu.SMEM),
            pl.BlockSpec((share * panels, tile), lambda c: (c, 0)),
        ],
        out_specs=[
            pl.BlockSpec((share, width), lambda c: (c, 0)),
            pl.BlockSpec((1, width, share), lambda c: (c, 0, 0)),
        ],
        out_shape=[
            jax.ShapeDtypeStruct((steps * share, width), BF16),
            jax.ShapeDtypeStruct((steps, width, share), BF16),
        ],
        compiler_params=params(),
        name="build_strip",
    )(live, cols, masks)


def stack_features(ids_ref, feature_refs, held):
    share = feature_refs[0].shape[0]
    for k, ref in enumerate(feature_refs):
        at = pl.multiple_of((ids_ref[1] ^ k) * share, share)
        held[pl.ds(at, share), :] = ref[...]


def sibling_sums_kernel(n, ids_ref, dense_ref, *refs):
    feature_refs, out_ref, held = refs[:n], refs[n], refs[n + 1]

    @pl.when(pl.program_id(0) == 0)
    def _():
        stack_features(ids_ref, feature_refs, held)

    out_ref[...] = dot(dense_ref[...], held[...]).astype(BF16)


def chip_sums_kernel(n, m, ids_ref, dense_ref, recv_ref, *refs):
    feature_refs, own_ref, out_refs, held = refs[:n], refs[n], refs[n + 1 : n + m], refs[n + m]
    step = pl.program_id(0)

    @pl.when(step == 0)
    def _():
        stack_features(ids_ref, feature_refs, held)

    total = dot(dense_ref[...], held[...]) + recv_ref[...].astype(F32)

    @pl.when(step == 0)
    def _():
        own_ref[...] = total

    for q in range(1, m):

        @pl.when(step == q)
        def _(q=q):
            out_refs[q - 1][...] = total.astype(BF16)


def sibling_sums(ids, dense, features, chips):
    share, width = features[0].shape
    n = len(features)
    return pl.pallas_call(
        functools.partial(sibling_sums_kernel, n),
        grid_spec=pltpu.PrefetchScalarGridSpec(
            num_scalar_prefetch=1,
            grid=(chips,),
            in_specs=[pl.BlockSpec((share, n * share), lambda q, ids: ((ids[0] ^ 1) ^ (2 * q), 0))]
            + [pl.BlockSpec((share, width), lambda q, ids: (0, 0))] * n,
            out_specs=pl.BlockSpec((share, width), lambda q, ids: (q, 0)),
            scratch_shapes=[pltpu.VMEM((n * share, width), BF16)],
        ),
        out_shape=jax.ShapeDtypeStruct((chips * share, width), BF16),
        compiler_params=params(),
        name="sibling_sums",
    )(ids, dense, *features)


def chip_sums(ids, dense, recv, features, chips):
    share, width = features[0].shape
    n = len(features)
    block = jax.ShapeDtypeStruct((share, width), BF16)
    fixed = pl.BlockSpec((share, width), lambda q, ids: (0, 0))
    return pl.pallas_call(
        functools.partial(chip_sums_kernel, n, chips),
        grid_spec=pltpu.PrefetchScalarGridSpec(
            num_scalar_prefetch=1,
            grid=(chips,),
            in_specs=[
                pl.BlockSpec((share, n * share), lambda q, ids: (ids[0] ^ (2 * q), 0)),
                pl.BlockSpec((share, width), lambda q, ids: (q, 0)),
            ]
            + [fixed] * n,
            out_specs=[fixed] * chips,
            scratch_shapes=[pltpu.VMEM((n * share, width), BF16)],
        ),
        out_shape=[jax.ShapeDtypeStruct((share, width), F32)] + [block] * (chips - 1),
        compiler_params=params(),
        name="chip_sums",
    )(ids, dense, recv, *features)


def rows_kernel(m, own_ref, ws_ref, wn_ref, bias_ref, deg_ref, cot_ref, agg_ref, *refs):
    recv_refs = refs[: m - 1]
    hidden_ref, dpre_ref, mean_ref, msg_ref, dbias_ref = refs[m - 1 :]
    agg = agg_ref[...]
    for ref in recv_refs:
        agg = agg + ref[...].astype(F32)
    deg = deg_ref[...]
    mean = (agg / deg).astype(BF16)
    mean_ref[...] = mean
    v = dot(own_ref[...], ws_ref[...]) + dot(mean, wn_ref[...]) + bias_ref[...]
    t = jnp.tanh(GELU_A * (v + GELU_B * (v * v * v)))
    hidden_ref[...] = (0.5 * v * (1.0 + t)).astype(BF16)
    slope = 0.5 * (1.0 + t) + 0.5 * v * (1.0 - t * t) * (GELU_A * (1.0 + 3.0 * GELU_B * v * v))
    dpre = cot_ref[...].astype(F32) * slope
    dpre_b = dpre.astype(BF16)
    dpre_ref[...] = dpre_b
    msg_ref[...] = (dot(dpre_b, wn_ref[...], CONTRACT_SECOND) / deg).astype(BF16)
    dbias_ref[...] = jnp.sum(dpre, axis=0, keepdims=True)


def rows_step(own, ws, wn, bias, deg, cot, agg, recvs):
    share, width = own.shape
    block = jax.ShapeDtypeStruct((share, width), BF16)
    m = len(recvs) + 1
    return pl.pallas_call(
        functools.partial(rows_kernel, m),
        in_specs=whole(7 + m - 1),
        out_specs=whole(5),
        out_shape=[block, block, block, block, jax.ShapeDtypeStruct((1, width), F32)],
        compiler_params=params(),
        name="rows_step",
    )(own, ws, wn, bias, deg, cot, agg, *recvs)


def local_grads_kernel(chips, scale, ids_ref, own_ref, mean_ref, dpre_ref, dbias_ref, away_ref, keep_ref, held):
    width = own_ref.shape[1]
    piece = width // (2 * chips)
    rows = 2 * piece + BIAS_ROWS
    dpre = dpre_ref[...]
    held[0:width, :] = dot(own_ref[...], dpre, CONTRACT_FIRST) * scale
    held[width : 2 * width, :] = dot(mean_ref[...], dpre, CONTRACT_FIRST) * scale
    dbias = jnp.broadcast_to(dbias_ref[...] * scale, (BIAS_ROWS, dbias_ref.shape[1]))
    for out_ref, base in ((away_ref, ids_ref[0] ^ 1), (keep_ref, ids_ref[0])):
        for q in range(chips):
            at = pl.multiple_of((base ^ (2 * q)) * piece, piece)
            out_ref[q * rows : q * rows + piece, :] = held[pl.ds(at, piece), :]
            out_ref[q * rows + piece : q * rows + 2 * piece, :] = held[pl.ds(width + at, piece), :]
            out_ref[q * rows + 2 * piece : (q + 1) * rows, :] = dbias


def local_grads(ids, own, mean, dpre, dbias, chips, scale):
    width = own.shape[1]
    rows = 2 * (width // (2 * chips)) + BIAS_ROWS
    out = jax.ShapeDtypeStruct((chips * rows, width), F32)
    return pl.pallas_call(
        functools.partial(local_grads_kernel, chips, scale),
        in_specs=[pl.BlockSpec(memory_space=pltpu.SMEM)] + whole(4),
        out_specs=whole(2),
        out_shape=[out, out],
        scratch_shapes=[pltpu.VMEM((2 * width, width), F32)],
        compiler_params=params(),
        name="local_grads",
    )(ids, own, mean, dpre, dbias)


def store_shard(out_ref, total):
    rows = total.shape[0]
    half = BIAS_ROWS // 2
    high = total.astype(BF16)
    tail = total[rows - BIAS_ROWS :, :]
    tail_high = tail.astype(BF16).astype(F32)
    index = lax.broadcasted_iota(jnp.int32, tail.shape, 0)
    mixed = jnp.where(index < half, tail_high, tail - tail_high)
    out_ref[0 : rows - BIAS_ROWS, :] = high[0 : rows - BIAS_ROWS, :]
    out_ref[rows - BIAS_ROWS :, :] = mixed.astype(BF16)


def load_shard(ref):
    value = ref[...].astype(F32)
    rows = value.shape[0]
    half = BIAS_ROWS // 2
    line = value[rows - BIAS_ROWS : rows - BIAS_ROWS + 1, :] + value[rows - half : rows - half + 1, :]
    return jnp.concatenate(
        [value[: rows - BIAS_ROWS, :], jnp.broadcast_to(line, (BIAS_ROWS, value.shape[1]))], axis=0
    )


def pair_grads_kernel(chips, keep_ref, recv_ref, own_ref, *out_refs):
    rows = own_ref.shape[0]
    own_ref[...] = keep_ref[0:rows, :] + recv_ref[0:rows, :]
    for q in range(1, chips):
        at = slice(q * rows, (q + 1) * rows)
        store_shard(out_refs[q - 1], keep_ref[at, :] + recv_ref[at, :])


def pair_grads(keep, recv, chips):
    rows, width = keep.shape[0] // chips, keep.shape[1]
    block = jax.ShapeDtypeStruct((rows, width), BF16)
    return pl.pallas_call(
        functools.partial(pair_grads_kernel, chips),
        in_specs=whole(2),
        out_specs=whole(chips),
        out_shape=[jax.ShapeDtypeStruct((rows, width), F32)] + [block] * (chips - 1),
        compiler_params=params(),
        name="pair_grads",
    )(keep, recv)


def panel_grads_kernel(n, own_ref, *refs):
    total = own_ref[...]
    for ref in refs[:n]:
        total = total + load_shard(ref)
    refs[n][...] = total
    store_shard(refs[n + 1], total)


def panel_grads(own, recvs):
    rows, width = own.shape
    return pl.pallas_call(
        functools.partial(panel_grads_kernel, len(recvs)),
        in_specs=whole(1 + len(recvs)),
        out_specs=whole(2),
        out_shape=[
            jax.ShapeDtypeStruct((rows, width), F32),
            jax.ShapeDtypeStruct((rows, width), BF16),
        ],
        compiler_params=params(),
        name="panel_grads",
    )(own, *recvs)


def all_grads_kernel(n, own_ref, *refs):
    total = own_ref[...]
    for ref in refs[:n]:
        total = total + load_shard(ref)
    rows = total.shape[0] - BIAS_ROWS
    refs[n][...] = total[:rows, :]
    refs[n + 1][...] = total[rows : rows + 1, :]


def all_grads(own, recvs):
    rows, width = own.shape
    return pl.pallas_call(
        functools.partial(all_grads_kernel, len(recvs)),
        in_specs=whole(1 + len(recvs)),
        out_specs=whole(2),
        out_shape=[
            jax.ShapeDtypeStruct((rows - BIAS_ROWS, width), F32),
            jax.ShapeDtypeStruct((1, width), F32),
        ],
        compiler_params=params(),
        name="all_grads",
    )(own, *recvs)


def place_grads_kernel(n, ids_ref, *refs):
    shard_refs, self_ref, neigh_ref = refs[:n], refs[n], refs[n + 1]
    piece = shard_refs[0].shape[0] // 2
    for k, ref in enumerate(shard_refs):
        at = pl.multiple_of((ids_ref[0] ^ k) * piece, piece)
        self_ref[pl.ds(at, piece), :] = ref[0:piece, :]
        neigh_ref[pl.ds(at, piece), :] = ref[piece : 2 * piece, :]


def place_grads(ids, shards):
    width = shards[0].shape[1]
    out = jax.ShapeDtypeStruct((width, width), F32)
    n = len(shards)
    return pl.pallas_call(
        functools.partial(place_grads_kernel, n),
        in_specs=[pl.BlockSpec(memory_space=pltpu.SMEM)] + whole(n),
        out_specs=whole(2),
        out_shape=[out, out],
        compiler_params=params(),
        name="place_grads",
    )(ids, *shards)


def back_kernel(n, first, offset, ids_ref, flip_ref, *refs):
    msg_refs = refs[:n]
    step = pl.program_id(0)
    if first:
        prior, total_ref = None, refs[n]
    else:
        prior, total_ref = refs[n], refs[-1]

    @pl.when(step == 0)
    def _():
        if first:
            total_ref[...] = jnp.zeros_like(total_ref)
        else:
            total_ref[...] = prior[...]

    for k in range(n):

        @pl.when(step == k)
        def _(k=k):
            total_ref[...] += dot(flip_ref[0], msg_refs[k][...])

    if not first:
        own_ref, out_refs = refs[n + 1], refs[n + 2 : -1]
        share = own_ref.shape[0]

        @pl.when(step == n - 1)
        def _():
            own_ref[...] = total_ref[pl.ds(pl.multiple_of(ids_ref[1] * share, share), share), :]
            for k, ref in enumerate(out_refs):
                at = pl.multiple_of((ids_ref[1] ^ (k + 1)) * share, share)
                ref[...] = total_ref[pl.ds(at, share), :].astype(BF16)


def back_sums(ids, flip, messages, offset, prior, panels):
    share, width = messages[0].shape
    n = len(messages)
    rows = panels * share
    fixed = pl.BlockSpec((share, width), lambda q, ids: (0, 0))
    total_spec = pl.BlockSpec((rows, width), lambda q, ids: (0, 0))
    first = prior is None
    total = jax.ShapeDtypeStruct((rows, width), F32)
    own = jax.ShapeDtypeStruct((share, width), F32)
    block = jax.ShapeDtypeStruct((share, width), BF16)
    return pl.pallas_call(
        functools.partial(back_kernel, n, first, offset),
        grid_spec=pltpu.PrefetchScalarGridSpec(
            num_scalar_prefetch=1,
            grid=(n,),
            in_specs=[
                pl.BlockSpec((1, rows, share), lambda q, ids: ((ids[0] ^ offset) ^ (2 * q), 0, 0))
            ]
            + [fixed] * n
            + ([] if first else [total_spec]),
            out_specs=total_spec if first else [fixed] * panels,
            scratch_shapes=[] if first else [pltpu.VMEM((rows, width), F32)],
        ),
        out_shape=total if first else [own] + [block] * (panels - 1),
        compiler_params=params(),
        name="back_sums_even" if first else "back_sums_odd",
    )(ids, flip, *messages, *([] if first else [prior]))


def feature_grads_kernel(n, dpre_ref, ws_ref, own_ref, *refs):
    total = own_ref[...]
    for ref in refs[:n]:
        total = total + ref[...].astype(F32)
    refs[n][...] = (total + dot(dpre_ref[...], ws_ref[...], CONTRACT_SECOND)).astype(BF16)


def feature_grads(dpre, ws, own, recvs):
    return pl.pallas_call(
        functools.partial(feature_grads_kernel, len(recvs)),
        in_specs=whole(3 + len(recvs)),
        out_specs=pl.BlockSpec(memory_space=pltpu.VMEM),
        out_shape=jax.ShapeDtypeStruct(dpre.shape, BF16),
        compiler_params=params(),
        name="feature_grads",
    )(dpre, ws, own, *recvs)


def per_device(
    features,
    self_weight,
    neigh_weight,
    out_bias,
    tile_masks,
    tile_live,
    tile_columns,
    node_degree,
    cotangent,
):
    row_devices = lax.axis_size("row")
    rep_devices = lax.axis_size("rep")
    chips = rep_devices // 2
    panel_rows, width = features.shape
    share = node_degree.shape[0]
    panels = tile_masks.shape[1]
    tile = tile_masks.shape[2]
    blocks = share // tile
    scale = 1.0 / math.sqrt(share * row_devices * rep_devices)
    rep, row = lax.axis_index("rep"), lax.axis_index("row")
    ids = jnp.stack([rep, row]).astype(jnp.int32)

    own = lax.dynamic_slice_in_dim(features, rep * share, share, 0)
    gathered = [own] + [xor_permute(own, "row", k) for k in range(1, row_devices)]
    dense, flip = build_strip(
        tile_masks.reshape(panel_rows * panels, tile), tile_live.T, tile_columns.T,
        panels, blocks, tile, rep_devices,
    )
    deg = jnp.broadcast_to(node_degree.astype(F32)[:, None], (share, width))

    away = sibling_sums(ids, dense, gathered, chips)
    sums = chip_sums(ids, dense, xor_permute(away, "rep", 1), gathered, chips)
    recvs = [xor_permute(sums[q], "rep", 2 * q) for q in range(1, chips)]
    hidden_out, dpre, mean, message, dbias = rows_step(
        own, self_weight, neigh_weight, out_bias[None, :], deg, cotangent, sums[0], recvs
    )

    even = [message] + [xor_permute(message, "rep", 2 * q) for q in range(1, chips)]
    odd = [xor_permute(value, "rep", 1) for value in even]
    half = back_sums(ids, flip, even, 0, None, panels)
    spread = back_sums(ids, flip, odd, 1, half, panels)

    grad_away, grad_keep = local_grads(ids, own, mean, dpre, dbias, chips, scale)
    pair = pair_grads(grad_keep, xor_permute(grad_away, "rep", 1), chips)
    panel, panel_b = panel_grads(
        pair[0], [xor_permute(pair[q], "rep", 2 * q) for q in range(1, chips)]
    )
    shard, grad_bias = all_grads(
        panel, [xor_permute(panel_b, "row", k) for k in range(1, row_devices)]
    )
    shards = [shard] + [xor_permute(shard, "rep", 2 * q) for q in range(1, chips)]
    others = [xor_permute(value, "rep", 1) for value in shards]
    ordered = [value for both in zip(shards, others) for value in both]
    grad_self, grad_neigh = place_grads(ids, ordered)

    arrived = [xor_permute(spread[k], "row", k) for k in range(1, row_devices)]
    grad_features = feature_grads(dpre, self_weight, spread[0], arrived)
    return (hidden_out, grad_features, grad_self, grad_neigh, grad_bias[0])


def solution(mesh):
    return jax.shard_map(
        per_device,
        mesh=mesh,
        in_specs=(
            P("row", None),
            P(),
            P(),
            P(),
            P("row", "rep", None),
            P("row", "rep"),
            P("row", "rep"),
            P(("row", "rep")),
            P(("row", "rep"), None),
        ),
        out_specs=(P(("row", "rep"), None), P(("row", "rep"), None), P(), P(), P()),
        check_vma=False,
    )
```

```python
import functools
import math

import jax
import jax.numpy as jnp
from jax import lax
from jax.experimental import pallas as pl
from jax.experimental.pallas import tpu as pltpu
from jax.sharding import PartitionSpec as P

BF16 = jnp.bfloat16
F32 = jnp.float32
BIAS_ROWS = 16
PIECES = 4
VMEM_LIMIT = 40 * 1024 * 1024
CONTRACT_FIRST = (((0,), (0,)), ((), ()))
CONTRACT_SECOND = (((1,), (1,)), ((), ()))
GELU_A = math.sqrt(2.0 / math.pi)
GELU_B = 0.044715


def dot(a, b, dims=(((1,), (0,)), ((), ()))):
    return lax.dot_general(a, b, dims, preferred_element_type=F32)


def params():
    return pltpu.CompilerParams(vmem_limit_bytes=VMEM_LIMIT)


def cost(flops, bytes_accessed):
    return pl.CostEstimate(flops=flops, bytes_accessed=bytes_accessed, transcendentals=0)


def whole(n):
    return [pl.BlockSpec(memory_space=pltpu.VMEM)] * n


def tree_sum(terms):
    terms = list(terms)
    while len(terms) > 1:
        terms = [a + b for a, b in zip(terms[::2], terms[1::2])]
    return terms[0]


def xor_permute(value, axis, k):
    return lax.ppermute(value, axis, [(i, i ^ k) for i in range(lax.axis_size(axis))])


def block_of(ids, p, chips):
    return (ids[0] ^ (1 - p // chips)) ^ (2 * (p % chips))


def strip_kernel(panels, blocks, tile, chips, ids_ref, live_ref, cols_ref, mask_ref, dense_ref, flip_ref):
    step = block_of(ids_ref, pl.program_id(0), chips)
    for j in range(blocks):
        i = step * blocks + j
        for s in range(panels):
            bits = mask_ref[pl.ds(j * tile * panels + s, tile, stride=panels), :].astype(F32)
            turned = bits.T
            live = live_ref[s, i] != 0
            col = cols_ref[s, i]
            for b in range(blocks):
                keep = jnp.where(live & (col == b), 1.0, 0.0).astype(F32)
                at = (s * blocks + b) * tile
                dense_ref[j * tile : (j + 1) * tile, at : at + tile] = (bits * keep).astype(BF16)
                flip_ref[at : at + tile, j * tile : (j + 1) * tile] = (turned * keep).astype(BF16)


def build_strip(ids, masks, live, cols, panels, blocks, tile, chips):
    share = blocks * tile
    width = panels * share
    rows = 2 * chips * share
    return pl.pallas_call(
        functools.partial(strip_kernel, panels, blocks, tile, chips),
        grid_spec=pltpu.PrefetchScalarGridSpec(
            num_scalar_prefetch=3,
            grid=(2 * chips,),
            in_specs=[
                pl.BlockSpec(
                    (share * panels, tile), lambda p, ids, live, cols: (block_of(ids, p, chips), 0)
                ),
            ],
            out_specs=[
                pl.BlockSpec((share, width), lambda p, ids, live, cols: (p, 0)),
                pl.BlockSpec((width, share), lambda p, ids, live, cols: (0, p)),
            ],
        ),
        out_shape=[
            jax.ShapeDtypeStruct((rows, width), BF16),
            jax.ShapeDtypeStruct((width, rows), BF16),
        ],
        compiler_params=params(),
        name="build_strip",
    )(ids, live, cols, masks)


def stack_features(ids_ref, feature_refs, held):
    share = feature_refs[0].shape[0]
    for k, ref in enumerate(feature_refs):
        at = pl.multiple_of((ids_ref[1] ^ k) * share, share)
        held[pl.ds(at, share), :] = ref[...]


def partial_sums_kernel(n, start, ids_ref, dense_ref, *refs):
    out_ref, held = refs[n], refs[n + 1]
    stack_features(ids_ref, refs[:n], held)
    rows = dense_ref[start : start + out_ref.shape[0], :]
    out_ref[...] = dot(rows, held[...]).astype(out_ref.dtype)


def partial_sums(ids, dense, features, part, dtype):
    share, width = features[0].shape
    n = len(features)
    rows = dense.shape[0] // 2
    return pl.pallas_call(
        functools.partial(partial_sums_kernel, n, part * rows),
        in_specs=[pl.BlockSpec(memory_space=pltpu.SMEM)] + whole(1 + n),
        out_specs=pl.BlockSpec(memory_space=pltpu.VMEM),
        out_shape=jax.ShapeDtypeStruct((rows, width), dtype),
        scratch_shapes=[pltpu.VMEM((n * share, width), BF16)],
        compiler_params=params(),
        name="keep_sums" if part else "away_sums",
    )(ids, dense, *features)


def chip_sums_kernel(m, keep_ref, recv_ref, own_ref, *out_refs):
    share = own_ref.shape[0]
    own_ref[...] = keep_ref[0:share, :] + recv_ref[0:share, :].astype(F32)
    for q in range(1, m):
        at = slice(q * share, (q + 1) * share)
        out_refs[q - 1][...] = (keep_ref[at, :] + recv_ref[at, :].astype(F32)).astype(BF16)


def chip_sums(keep, received, chips):
    share, width = keep.shape[0] // chips, keep.shape[1]
    block = jax.ShapeDtypeStruct((share, width), BF16)
    return pl.pallas_call(
        functools.partial(chip_sums_kernel, chips),
        in_specs=whole(2),
        out_specs=whole(chips),
        out_shape=[jax.ShapeDtypeStruct((share, width), F32)] + [block] * (chips - 1),
        compiler_params=params(),
        name="chip_sums",
    )(keep, received)


def rows_kernel(m, scale, ids_ref, own_ref, ws_ref, wn_ref, bias_ref, deg_ref, cot_ref, agg_ref, *refs):
    hidden_ref, dpre_ref, msg_ref, away_ref, keep_ref = refs[m - 1 :]
    width = own_ref.shape[1]
    agg = agg_ref[...]
    for ref in refs[: m - 1]:
        agg = agg + ref[...].astype(F32)
    deg = deg_ref[...]
    mean = (agg / deg).astype(BF16)
    v = dot(own_ref[...], ws_ref[...]) + dot(mean, wn_ref[...]) + bias_ref[...]
    t = jnp.tanh(GELU_A * (v + GELU_B * (v * v * v)))
    hidden_ref[...] = (0.5 * v * (1.0 + t)).astype(BF16)
    slope = 0.5 * (1.0 + t) + 0.5 * v * (1.0 - t * t) * (GELU_A * (1.0 + 3.0 * GELU_B * v * v))
    dpre = cot_ref[...].astype(F32) * slope
    dpre_b = dpre.astype(BF16)
    dpre_ref[...] = dpre_b
    msg_ref[...] = (dot(dpre_b, wn_ref[...], CONTRACT_SECOND) / deg).astype(BF16)
    dbias = jnp.broadcast_to(jnp.sum(dpre, axis=0, keepdims=True) * scale, (BIAS_ROWS, width))
    away_ref[width:, :] = dbias
    keep_ref[width:, :] = dbias
    first = (ids_ref[0] & 1) == 0
    mine = jnp.where(first, own_ref[...], mean)
    other = jnp.where(first, mean, own_ref[...])
    keep_ref[0:width, :] = dot(mine, dpre_b, CONTRACT_FIRST) * scale
    away_ref[0:width, :] = dot(other, dpre_b, CONTRACT_FIRST) * scale


def rows_step(ids, own, ws, wn, bias, deg, cot, agg, recvs, scale):
    share, width = own.shape
    block = jax.ShapeDtypeStruct((share, width), BF16)
    grads = jax.ShapeDtypeStruct((width + BIAS_ROWS, width), F32)
    m = len(recvs) + 1
    return pl.pallas_call(
        functools.partial(rows_kernel, m, scale),
        in_specs=[pl.BlockSpec(memory_space=pltpu.SMEM)] + whole(7 + m - 1),
        out_specs=whole(5),
        out_shape=[block, block, block, grads, grads],
        compiler_params=params(),
        name="rows_step",
    )(ids, own, ws, wn, bias, deg, cot, agg, *recvs)


def store_rounded(out_ref, total):
    rows = total.shape[0]
    tail = total[rows - BIAS_ROWS :, :]
    tail_high = tail.astype(BF16).astype(F32)
    index = lax.broadcasted_iota(jnp.int32, tail.shape, 0)
    mixed = jnp.where(index < BIAS_ROWS // 2, tail_high, tail - tail_high)
    out_ref[0 : rows - BIAS_ROWS, :] = total[0 : rows - BIAS_ROWS, :].astype(BF16)
    out_ref[rows - BIAS_ROWS :, :] = mixed.astype(BF16)


def load_sum(refs):
    rows = refs[0].shape[0]
    body = tree_sum(ref[0 : rows - BIAS_ROWS, :].astype(F32) for ref in refs)
    tail = tree_sum(ref[rows - BIAS_ROWS :, :].astype(F32) for ref in refs)
    return body, tail[0:1, :] + tail[BIAS_ROWS // 2 : BIAS_ROWS // 2 + 1, :]


def pair_grads_kernel(keep_ref, recv_ref, out_ref):
    store_rounded(out_ref, keep_ref[...] + recv_ref[...])


def pair_grads(keep, recv):
    return pl.pallas_call(
        pair_grads_kernel,
        in_specs=whole(2),
        out_specs=pl.BlockSpec(memory_space=pltpu.VMEM),
        out_shape=jax.ShapeDtypeStruct(keep.shape, BF16),
        compiler_params=params(),
        name="pair_grads",
    )(keep, recv)


def line_grads_kernel(n, *refs):
    body, line = load_sum(refs[:n])
    tail = jnp.broadcast_to(line, (BIAS_ROWS, line.shape[1]))
    store_rounded(refs[-1], jnp.concatenate([body, tail], axis=0))


def line_grads(parts, after=()):
    n = len(parts)
    return pl.pallas_call(
        functools.partial(line_grads_kernel, n),
        in_specs=whole(n) + [pl.BlockSpec(memory_space=pl.ANY)] * len(after),
        out_specs=pl.BlockSpec(memory_space=pltpu.VMEM),
        out_shape=jax.ShapeDtypeStruct(parts[0].shape, BF16),
        compiler_params=params(),
        name="line_grads",
    )(*parts, *after)


def all_grads_kernel(n, *refs):
    body, line = load_sum(refs[:n])
    rows = refs[n].shape[0]
    for i in range(PIECES):
        refs[n + i][...] = body[i * rows : (i + 1) * rows, :]
    refs[n + PIECES][...] = body
    refs[n + PIECES + 1][...] = line


def all_grads(parts):
    n = len(parts)
    rows, width = parts[0].shape
    return pl.pallas_call(
        functools.partial(all_grads_kernel, n),
        in_specs=whole(n),
        out_specs=whole(PIECES + 2),
        out_shape=[jax.ShapeDtypeStruct(((rows - BIAS_ROWS) // PIECES, width), F32)] * PIECES
        + [
            jax.ShapeDtypeStruct((rows - BIAS_ROWS, width), F32),
            jax.ShapeDtypeStruct((1, width), F32),
        ],
        compiler_params=params(),
        name="all_grads",
    )(*parts)


def place_grads_kernel(ids_ref, mine_ref, *refs):
    other_refs, (after_ref, self_ref, neigh_ref) = refs[:-3], refs[-3:]
    first = (ids_ref[0] & 1) == 0
    rows = other_refs[0].shape[0]
    for i, ref in enumerate(other_refs):
        at = slice(i * rows, (i + 1) * rows)
        self_ref[at, :] = jnp.where(first, mine_ref[at, :], ref[...])
        neigh_ref[at, :] = jnp.where(first, ref[...], mine_ref[at, :])


def place_grads(ids, mine, others, after):
    out = jax.ShapeDtypeStruct(mine.shape, F32)
    return pl.pallas_call(
        place_grads_kernel,
        in_specs=[pl.BlockSpec(memory_space=pltpu.SMEM)]
        + whole(1 + len(others))
        + [pl.BlockSpec(memory_space=pl.ANY)],
        out_specs=whole(2),
        out_shape=[out, out],
        compiler_params=params(),
        name="place_grads",
    )(ids, mine, *others, after)


def stack_messages(message_refs, held):
    share = message_refs[0].shape[0]
    for q, ref in enumerate(message_refs):
        held[q * share : (q + 1) * share, :] = ref[...]


def back_even_kernel(n, flip_ref, *refs):
    out_ref, held = refs[n], refs[n + 1]
    stack_messages(refs[:n], held)
    out_ref[...] = dot(flip_ref[:, held.shape[0] :], held[...])


def back_even(flip, messages):
    share, width = messages[0].shape
    n = len(messages)
    return pl.pallas_call(
        functools.partial(back_even_kernel, n),
        in_specs=whole(1 + n),
        out_specs=pl.BlockSpec(memory_space=pltpu.VMEM),
        out_shape=jax.ShapeDtypeStruct((flip.shape[0], width), F32),
        scratch_shapes=[pltpu.VMEM((n * share, width), BF16)],
        compiler_params=params(),
        name="back_even",
    )(flip, *messages)


def back_odd_kernel(n, ids_ref, flip_ref, prior_ref, *refs):
    own_ref, out_refs, held, total = refs[n], refs[n + 1 : -2], refs[-2], refs[-1]
    share = own_ref.shape[0]
    stack_messages(refs[:n], held)
    total[...] = prior_ref[...] + dot(flip_ref[:, 0 : held.shape[0]], held[...])
    own_ref[...] = total[pl.ds(pl.multiple_of(ids_ref[1] * share, share), share), :]
    for k, ref in enumerate(out_refs):
        at = pl.multiple_of((ids_ref[1] ^ (k + 1)) * share, share)
        ref[...] = total[pl.ds(at, share), :].astype(BF16)


def back_odd(ids, flip, prior, messages, panels):
    share, width = messages[0].shape
    n = len(messages)
    block = jax.ShapeDtypeStruct((share, width), BF16)
    return pl.pallas_call(
        functools.partial(back_odd_kernel, n),
        in_specs=[pl.BlockSpec(memory_space=pltpu.SMEM)] + whole(2 + n),
        out_specs=whole(panels),
        out_shape=[jax.ShapeDtypeStruct((share, width), F32)] + [block] * (panels - 1),
        scratch_shapes=[pltpu.VMEM((n * share, width), BF16), pltpu.VMEM(prior.shape, F32)],
        compiler_params=params(),
        name="back_odd",
    )(ids, flip, prior, *messages)


def feature_grads_kernel(n, dpre_ref, ws_ref, own_ref, *refs):
    total = own_ref[...]
    for ref in refs[:n]:
        total = total + ref[...].astype(F32)
    refs[n][...] = (total + dot(dpre_ref[...], ws_ref[...], CONTRACT_SECOND)).astype(BF16)


def feature_grads(dpre, ws, own, recvs):
    return pl.pallas_call(
        functools.partial(feature_grads_kernel, len(recvs)),
        in_specs=whole(3 + len(recvs)),
        out_specs=pl.BlockSpec(memory_space=pltpu.VMEM),
        out_shape=jax.ShapeDtypeStruct(dpre.shape, BF16),
        compiler_params=params(),
        name="feature_grads",
    )(dpre, ws, own, *recvs)


def per_device(
    features,
    self_weight,
    neigh_weight,
    out_bias,
    tile_masks,
    tile_live,
    tile_columns,
    node_degree,
    cotangent,
):
    row_devices = lax.axis_size("row")
    rep_devices = lax.axis_size("rep")
    chips = rep_devices // 2
    panel_rows, width = features.shape
    share = node_degree.shape[0]
    panels = tile_masks.shape[1]
    tile = tile_masks.shape[2]
    blocks = share // tile
    scale = 1.0 / math.sqrt(share * row_devices * rep_devices)
    rep, row = lax.axis_index("rep"), lax.axis_index("row")
    ids = jnp.stack([rep, row]).astype(jnp.int32)

    own = lax.dynamic_slice_in_dim(features, rep * share, share, 0)
    gathered = [own] + [xor_permute(own, "row", k) for k in range(1, row_devices)]
    dense, flip = build_strip(
        ids, tile_masks.reshape(panel_rows * panels, tile), tile_live.T, tile_columns.T,
        panels, blocks, tile, chips,
    )
    deg = jnp.broadcast_to(node_degree.astype(F32)[:, None], (share, width))

    away = partial_sums(ids, dense, gathered, 0, BF16)
    keep = partial_sums(ids, dense, gathered, 1, F32)
    sums = chip_sums(keep, xor_permute(away, "rep", 1), chips)
    recvs = [xor_permute(sums[q], "rep", 2 * q) for q in range(1, chips)]
    hidden_out, dpre, message, grad_away, grad_keep = rows_step(
        ids, own, self_weight, neigh_weight, out_bias[None, :], deg, cotangent, sums[0], recvs, scale
    )

    even = [message] + [xor_permute(message, "rep", 2 * q) for q in range(1, chips)]
    odd = [xor_permute(value, "rep", 1) for value in even]
    half = back_even(flip, even)
    spread = back_odd(ids, flip, half, odd, panels)
    token = spread[0]

    line = pair_grads(grad_keep, xor_permute(grad_away, "rep", 1))
    k = 1
    while k < row_devices:
        after = [token] if 2 * k == row_devices else []
        line = line_grads([line, xor_permute(line, "row", k)], after)
        k *= 2
    *pieces, mine, grad_bias = all_grads(
        [line] + [xor_permute(line, "rep", 2 * q) for q in range(1, chips)]
    )
    arrived = [xor_permute(spread[k], "row", k) for k in range(1, row_devices)]
    grad_features = feature_grads(dpre, self_weight, spread[0], arrived)
    late = xor_permute(grad_features, "rep", 1)
    others = [xor_permute(piece, "rep", 1) for piece in pieces]
    grad_self, grad_neigh = place_grads(ids, mine, others, late)
    return (hidden_out, grad_features, grad_self, grad_neigh, grad_bias[0])


def solution(mesh):
    return jax.shard_map(
        per_device,
        mesh=mesh,
        in_specs=(
            P("row", None),
            P(),
            P(),
            P(),
            P("row", "rep", None),
            P("row", "rep"),
            P("row", "rep"),
            P(("row", "rep")),
            P(("row", "rep"), None),
        ),
        out_specs=(P(("row", "rep"), None), P(("row", "rep"), None), P(), P(), P()),
        check_vma=False,
    )
```

```python
import functools
import math

import jax
import jax.numpy as jnp
from jax import lax
from jax.experimental import pallas as pl
from jax.experimental.pallas import tpu as pltpu
from jax.sharding import PartitionSpec as P

BF16 = jnp.bfloat16
F32 = jnp.float32
BIAS_ROWS = 16
SPACER_ROWS = 576
VMEM_LIMIT = 40 * 1024 * 1024
CONTRACT_FIRST = (((0,), (0,)), ((), ()))
CONTRACT_SECOND = (((1,), (1,)), ((), ()))
GELU_A = math.sqrt(2.0 / math.pi)
GELU_B = 0.044715


def dot(a, b, dims=(((1,), (0,)), ((), ()))):
    return lax.dot_general(a, b, dims, preferred_element_type=F32)


def params():
    return pltpu.CompilerParams(vmem_limit_bytes=VMEM_LIMIT)


def cost(flops, bytes_accessed):
    return pl.CostEstimate(flops=flops, bytes_accessed=bytes_accessed, transcendentals=0)


def whole(n):
    return [pl.BlockSpec(memory_space=pltpu.VMEM)] * n


def tree_sum(terms):
    terms = list(terms)
    while len(terms) > 1:
        terms = [a + b for a, b in zip(terms[::2], terms[1::2])]
    return terms[0]


def xor_permute(value, axis, k):
    return lax.ppermute(value, axis, [(i, i ^ k) for i in range(lax.axis_size(axis))])


def block_of(ids, p, chips):
    return (ids[0] ^ (1 - p // chips)) ^ (2 * (p % chips))


def strip_kernel(panels, blocks, tile, chips, ids_ref, live_ref, cols_ref, mask_ref, dense_ref, flip_ref):
    step = block_of(ids_ref, pl.program_id(0), chips)
    for j in range(blocks):
        i = step * blocks + j
        for s in range(panels):
            bits = mask_ref[pl.ds(j * tile * panels + s, tile, stride=panels), :].astype(F32)
            turned = bits.T
            live = live_ref[s, i] != 0
            col = cols_ref[s, i]
            for b in range(blocks):
                keep = jnp.where(live & (col == b), 1.0, 0.0).astype(F32)
                at = (s * blocks + b) * tile
                dense_ref[j * tile : (j + 1) * tile, at : at + tile] = (bits * keep).astype(BF16)
                flip_ref[at : at + tile, j * tile : (j + 1) * tile] = (turned * keep).astype(BF16)


def build_strip(ids, masks, live, cols, panels, blocks, tile, chips):
    share = blocks * tile
    width = panels * share
    rows = 2 * chips * share
    return pl.pallas_call(
        functools.partial(strip_kernel, panels, blocks, tile, chips),
        grid_spec=pltpu.PrefetchScalarGridSpec(
            num_scalar_prefetch=3,
            grid=(2 * chips,),
            in_specs=[
                pl.BlockSpec(
                    (share * panels, tile), lambda p, ids, live, cols: (block_of(ids, p, chips), 0)
                ),
            ],
            out_specs=[
                pl.BlockSpec((share, width), lambda p, ids, live, cols: (p, 0)),
                pl.BlockSpec((width, share), lambda p, ids, live, cols: (0, p)),
            ],
        ),
        out_shape=[
            jax.ShapeDtypeStruct((rows, width), BF16),
            jax.ShapeDtypeStruct((width, rows), BF16),
        ],
        compiler_params=params(),
        name="build_strip",
    )(ids, live, cols, masks)


def stack_features(ids_ref, feature_refs, held):
    share = feature_refs[0].shape[0]
    for k, ref in enumerate(feature_refs):
        at = pl.multiple_of((ids_ref[1] ^ k) * share, share)
        held[pl.ds(at, share), :] = ref[...]


def away_sums_kernel(n, start, ids_ref, dense_ref, *refs):
    out_ref, held_ref = refs[n:]
    stack_features(ids_ref, refs[:n], held_ref)
    rows = dense_ref[start : start + out_ref.shape[0], :]
    out_ref[...] = dot(rows, held_ref[...]).astype(BF16)


def away_far_sums(ids, dense, features, first):
    share, width = features[0].shape
    n = len(features)
    return pl.pallas_call(
        functools.partial(away_sums_kernel, n, first * share),
        in_specs=[pl.BlockSpec(memory_space=pltpu.SMEM)] + whole(1 + n),
        out_specs=whole(2),
        out_shape=[
            jax.ShapeDtypeStruct((share, width), BF16),
            jax.ShapeDtypeStruct((n * share, width), BF16),
        ],
        compiler_params=params(),
        name="away_far",
    )(ids, dense, *features)


def away_near_kernel(dense_ref, held_ref, *out_refs):
    share = out_refs[0].shape[0]
    total = dot(dense_ref[0 : len(out_refs) * share, :], held_ref[...])
    for q, ref in enumerate(out_refs):
        ref[...] = total[q * share : (q + 1) * share, :].astype(BF16)


def away_near_sums(dense, held, count, share):
    return pl.pallas_call(
        away_near_kernel,
        in_specs=whole(2),
        out_specs=whole(count),
        out_shape=[jax.ShapeDtypeStruct((share, held.shape[1]), BF16)] * count,
        compiler_params=params(),
        name="away_near",
    )(dense, held)


def chip_sums_kernel(start, dense_ref, held_ref, *refs):
    m = len(refs) // 2
    share = refs[0].shape[0]
    total = dot(dense_ref[start : start + m * share, :], held_ref[...])
    for q in range(m):
        part = total[q * share : (q + 1) * share, :] + refs[q][...].astype(F32)
        refs[m + q][...] = part.astype(refs[m + q].dtype)


def chip_sums(dense, received, held, first, dtypes, name):
    share, width = received[0].shape
    return pl.pallas_call(
        functools.partial(chip_sums_kernel, first * share),
        in_specs=whole(2 + len(received)),
        out_specs=whole(len(received)),
        out_shape=[jax.ShapeDtypeStruct((share, width), dtype) for dtype in dtypes],
        compiler_params=params(),
        name=name,
    )(dense, held, *received)


def add_far_kernel(own_ref, far_ref, out_ref):
    out_ref[...] = own_ref[...] + far_ref[...].astype(F32)


def add_far(own, far):
    return pl.pallas_call(
        add_far_kernel,
        in_specs=whole(2),
        out_specs=pl.BlockSpec(memory_space=pltpu.VMEM),
        out_shape=jax.ShapeDtypeStruct(own.shape, F32),
        cost_estimate=cost(10000000, 10**6),
        compiler_params=params(),
        name="add_far",
    )(own, far)


def rows_kernel(m, scale, ids_ref, own_ref, ws_ref, wn_ref, bias_ref, deg_ref, cot_ref, agg_ref, *refs):
    hidden_ref, dpre_ref, msg_ref, away_ref, keep_ref = refs[m - 1 :]
    width = own_ref.shape[1]
    agg = agg_ref[...]
    for ref in refs[: m - 1]:
        agg = agg + ref[...].astype(F32)
    deg = deg_ref[...]
    mean = (agg / deg).astype(BF16)
    v = dot(own_ref[...], ws_ref[...]) + dot(mean, wn_ref[...]) + bias_ref[...]
    t = jnp.tanh(GELU_A * (v + GELU_B * (v * v * v)))
    hidden_ref[...] = (0.5 * v * (1.0 + t)).astype(BF16)
    slope = 0.5 * (1.0 + t) + 0.5 * v * (1.0 - t * t) * (GELU_A * (1.0 + 3.0 * GELU_B * v * v))
    dpre = cot_ref[...].astype(F32) * slope
    dpre_b = dpre.astype(BF16)
    dpre_ref[...] = dpre_b
    msg_ref[...] = (dot(dpre_b, wn_ref[...], CONTRACT_SECOND) / deg).astype(BF16)
    dbias = jnp.broadcast_to(jnp.sum(dpre, axis=0, keepdims=True) * scale, (BIAS_ROWS, width))
    away_ref[width:, :] = dbias
    keep_ref[width:, :] = dbias
    first = (ids_ref[0] & 1) == 0
    mine = jnp.where(first, own_ref[...], mean)
    other = jnp.where(first, mean, own_ref[...])
    keep_ref[0:width, :] = dot(mine, dpre_b, CONTRACT_FIRST) * scale
    away_ref[0:width, :] = dot(other, dpre_b, CONTRACT_FIRST) * scale


def rows_step(ids, own, ws, wn, bias, deg, cot, agg, recvs, scale):
    share, width = own.shape
    block = jax.ShapeDtypeStruct((share, width), BF16)
    grads = jax.ShapeDtypeStruct((width + BIAS_ROWS, width), F32)
    m = len(recvs) + 1
    return pl.pallas_call(
        functools.partial(rows_kernel, m, scale),
        in_specs=[pl.BlockSpec(memory_space=pltpu.SMEM)] + whole(7 + m - 1),
        out_specs=whole(5),
        out_shape=[block, block, block, grads, grads],
        compiler_params=params(),
        name="rows_step",
    )(ids, own, ws, wn, bias, deg, cot, agg, *recvs)


def store_rounded(out_ref, total):
    rows = total.shape[0]
    tail = total[rows - BIAS_ROWS :, :]
    tail_high = tail.astype(BF16).astype(F32)
    index = lax.broadcasted_iota(jnp.int32, tail.shape, 0)
    mixed = jnp.where(index < BIAS_ROWS // 2, tail_high, tail - tail_high)
    out_ref[0 : rows - BIAS_ROWS, :] = total[0 : rows - BIAS_ROWS, :].astype(BF16)
    out_ref[rows - BIAS_ROWS :, :] = mixed.astype(BF16)


def load_sum(refs):
    rows = refs[0].shape[0]
    body = tree_sum(ref[0 : rows - BIAS_ROWS, :].astype(F32) for ref in refs)
    tail = tree_sum(ref[rows - BIAS_ROWS :, :].astype(F32) for ref in refs)
    return body, tail[0:1, :] + tail[BIAS_ROWS // 2 : BIAS_ROWS // 2 + 1, :]


def pair_grads_kernel(keep_ref, recv_ref, out_ref):
    store_rounded(out_ref, keep_ref[...] + recv_ref[...])


def pair_grads(keep, recv):
    return pl.pallas_call(
        pair_grads_kernel,
        in_specs=whole(2),
        out_specs=pl.BlockSpec(memory_space=pltpu.VMEM),
        out_shape=jax.ShapeDtypeStruct(keep.shape, BF16),
        compiler_params=params(),
        name="pair_grads",
    )(keep, recv)


def line_grads_kernel(n, *refs):
    body, line = load_sum(refs[:n])
    tail = jnp.broadcast_to(line, (BIAS_ROWS, line.shape[1]))
    store_rounded(refs[-1], jnp.concatenate([body, tail], axis=0))


def line_grads(parts):
    n = len(parts)
    return pl.pallas_call(
        functools.partial(line_grads_kernel, n),
        in_specs=whole(n),
        out_specs=pl.BlockSpec(memory_space=pltpu.VMEM),
        out_shape=jax.ShapeDtypeStruct(parts[0].shape, BF16),
        compiler_params=params(),
        name="line_grads",
    )(*parts)


def all_grads_kernel(n, *refs):
    body, line = load_sum(refs[:n])
    refs[n][...] = body
    refs[n + 1][...] = line


def all_grads(parts):
    n = len(parts)
    rows, width = parts[0].shape
    return pl.pallas_call(
        functools.partial(all_grads_kernel, n),
        in_specs=whole(n),
        out_specs=whole(2),
        out_shape=[
            jax.ShapeDtypeStruct((rows - BIAS_ROWS, width), F32),
            jax.ShapeDtypeStruct((1, width), F32),
        ],
        compiler_params=params(),
        name="all_grads",
    )(*parts)


def place_grads_kernel(ids_ref, mine_ref, other_ref, line_ref, after_ref, self_ref, neigh_ref, bias_ref):
    first = (ids_ref[0] & 1) == 0
    self_ref[...] = jnp.where(first, mine_ref[...], other_ref[...])
    neigh_ref[...] = jnp.where(first, other_ref[...], mine_ref[...])
    bias_ref[...] = line_ref[...]


def place_grads(ids, mine, other, line, after):
    out = jax.ShapeDtypeStruct(mine.shape, F32)
    return pl.pallas_call(
        place_grads_kernel,
        in_specs=[pl.BlockSpec(memory_space=pltpu.SMEM)]
        + whole(3)
        + [pl.BlockSpec(memory_space=pl.ANY)],
        out_specs=whole(3),
        out_shape=[out, out, jax.ShapeDtypeStruct(line.shape, F32)],
        compiler_params=params(),
        name="place_grads",
    )(ids, mine, other, line, after)


def back_kernel(n, ids_ref, flip_ref, *refs):
    own_ref, out_refs, held, total = refs[n], refs[n + 1 : -2], refs[-2], refs[-1]
    share = own_ref.shape[0]
    for q, ref in enumerate(refs[:n]):
        held[q * share : (q + 1) * share, :] = ref[...]
    total[...] = dot(flip_ref[...], held[...])
    own_ref[...] = total[pl.ds(pl.multiple_of(ids_ref[1] * share, share), share), :]
    for k, ref in enumerate(out_refs):
        at = pl.multiple_of((ids_ref[1] ^ (k + 1)) * share, share)
        ref[...] = total[pl.ds(at, share), :].astype(BF16)


def back_sums(ids, flip, messages, panels):
    share, width = messages[0].shape
    n = len(messages)
    block = jax.ShapeDtypeStruct((share, width), BF16)
    return pl.pallas_call(
        functools.partial(back_kernel, n),
        in_specs=[pl.BlockSpec(memory_space=pltpu.SMEM)] + whole(1 + n),
        out_specs=whole(panels),
        out_shape=[jax.ShapeDtypeStruct((share, width), F32)] + [block] * (panels - 1),
        scratch_shapes=[
            pltpu.VMEM((n * share, width), BF16),
            pltpu.VMEM((panels * share, width), F32),
        ],
        compiler_params=params(),
        name="back_sums",
    )(ids, flip, *messages)


def feature_grads_kernel(n, dpre_ref, ws_ref, own_ref, *refs):
    total = own_ref[...]
    for ref in refs[:n]:
        total = total + ref[...].astype(F32)
    total = total + dot(dpre_ref[...], ws_ref[...], CONTRACT_SECOND)
    refs[n][...] = total.astype(BF16)
    refs[n + 1][...] = jnp.zeros_like(refs[n + 1])


def feature_grads(dpre, ws, own, recvs):
    return pl.pallas_call(
        functools.partial(feature_grads_kernel, len(recvs)),
        in_specs=whole(3 + len(recvs)),
        out_specs=whole(2),
        out_shape=[jax.ShapeDtypeStruct(dpre.shape, BF16), jax.ShapeDtypeStruct((SPACER_ROWS, dpre.shape[1]), BF16)],
        compiler_params=params(),
        name="feature_grads",
    )(dpre, ws, own, *recvs)


def per_device(
    features,
    self_weight,
    neigh_weight,
    out_bias,
    tile_masks,
    tile_live,
    tile_columns,
    node_degree,
    cotangent,
):
    row_devices = lax.axis_size("row")
    rep_devices = lax.axis_size("rep")
    chips = rep_devices // 2
    panel_rows, width = features.shape
    share = node_degree.shape[0]
    panels = tile_masks.shape[1]
    tile = tile_masks.shape[2]
    blocks = share // tile
    scale = 1.0 / math.sqrt(share * row_devices * rep_devices)
    rep, row = lax.axis_index("rep"), lax.axis_index("row")
    ids = jnp.stack([rep, row]).astype(jnp.int32)

    own = lax.dynamic_slice_in_dim(features, rep * share, share, 0)
    gathered = [own] + [xor_permute(own, "row", k) for k in range(1, row_devices)]
    dense, flip = build_strip(
        ids, tile_masks.reshape(panel_rows * panels, tile), tile_live.T, tile_columns.T,
        panels, blocks, tile, chips,
    )
    deg = jnp.broadcast_to(node_degree.astype(F32)[:, None], (share, width))

    last = chips - 1
    away_far, held = away_far_sums(ids, dense, gathered, last)
    away = away_near_sums(dense, held, last, share)
    (far,) = chip_sums(dense, [xor_permute(away_far, "rep", 1)], held, chips + last, [BF16], "chip_far")
    far = xor_permute(far, "rep", 2 * last)
    sums = chip_sums(
        dense, [xor_permute(value, "rep", 1) for value in away], held, chips,
        [F32] + [BF16] * (last - 1), "chip_near",
    )
    recvs = [xor_permute(sums[q], "rep", 2 * q) for q in reversed(range(1, last))]
    agg = add_far(sums[0], far)
    hidden_out, dpre, message, grad_away, grad_keep = rows_step(
        ids, own, self_weight, neigh_weight, out_bias[None, :], deg, cotangent, agg, recvs, scale
    )

    even = [xor_permute(message, "rep", 2 * q) for q in reversed(range(1, chips))]
    even = [message] + even[::-1]
    odd = [xor_permute(value, "rep", 1) for value in even]
    spread = back_sums(ids, flip, odd + even, panels)

    line = pair_grads(grad_keep, xor_permute(grad_away, "rep", 1))
    k = 1
    while k < row_devices:
        line = line_grads([line, xor_permute(line, "row", k)])
        k *= 2
    arrived = [xor_permute(spread[k], "row", k) for k in range(1, row_devices)]
    grad_features, spacer = feature_grads(dpre, self_weight, spread[0], arrived)
    late = xor_permute(spacer, "rep", 1)
    mine, bias_line = all_grads(
        [line] + [xor_permute(line, "rep", 2 * q) for q in range(1, chips)]
    )
    grad_self, grad_neigh, grad_bias = place_grads(
        ids, mine, xor_permute(mine, "rep", 1), bias_line, late
    )
    return (hidden_out, grad_features, grad_self, grad_neigh, grad_bias[0])


def solution(mesh):
    return jax.shard_map(
        per_device,
        mesh=mesh,
        in_specs=(
            P("row", None),
            P(),
            P(),
            P(),
            P("row", "rep", None),
            P("row", "rep"),
            P("row", "rep"),
            P(("row", "rep")),
            P(("row", "rep"), None),
        ),
        out_specs=(P(("row", "rep"), None), P(("row", "rep"), None), P(), P(), P()),
        check_vma=False,
    )
```

```python
import functools
import math

import jax
import jax.numpy as jnp
from jax import lax
from jax.experimental import pallas as pl
from jax.experimental.pallas import tpu as pltpu
from jax.sharding import PartitionSpec as P

BF16 = jnp.bfloat16
F32 = jnp.float32
BIAS_ROWS = 16
SPACER_ROWS = 576
FAR_ROWS = 32
VMEM_LIMIT = 40 * 1024 * 1024
CONTRACT_FIRST = (((0,), (0,)), ((), ()))
CONTRACT_SECOND = (((1,), (1,)), ((), ()))
GELU_A = math.sqrt(2.0 / math.pi)
GELU_B = 0.044715


def dot(a, b, dims=(((1,), (0,)), ((), ()))):
    return lax.dot_general(a, b, dims, preferred_element_type=F32)


def params():
    return pltpu.CompilerParams(vmem_limit_bytes=VMEM_LIMIT)


def cost(flops, bytes_accessed):
    return pl.CostEstimate(flops=flops, bytes_accessed=bytes_accessed, transcendentals=0)


def whole(n):
    return [pl.BlockSpec(memory_space=pltpu.VMEM)] * n


def tree_sum(terms):
    terms = list(terms)
    while len(terms) > 1:
        terms = [a + b for a, b in zip(terms[::2], terms[1::2])]
    return terms[0]


def xor_permute(value, axis, k):
    return lax.ppermute(value, axis, [(i, i ^ k) for i in range(lax.axis_size(axis))])


def block_of(ids, p, chips):
    return (ids[0] ^ (1 - p // chips)) ^ (2 * (p % chips))


def strip_kernel(panels, blocks, tile, chips, ids_ref, live_ref, cols_ref, mask_ref, dense_ref, flip_ref):
    step = block_of(ids_ref, pl.program_id(0), chips)
    for j in range(blocks):
        i = step * blocks + j
        for s in range(panels):
            bits = mask_ref[pl.ds(j * tile * panels + s, tile, stride=panels), :].astype(F32)
            turned = bits.T
            live = live_ref[s, i] != 0
            col = cols_ref[s, i]
            for b in range(blocks):
                keep = jnp.where(live & (col == b), 1.0, 0.0).astype(F32)
                at = (s * blocks + b) * tile
                dense_ref[j * tile : (j + 1) * tile, at : at + tile] = (bits * keep).astype(BF16)
                flip_ref[at : at + tile, j * tile : (j + 1) * tile] = (turned * keep).astype(BF16)


def build_strip(ids, masks, live, cols, panels, blocks, tile, chips):
    share = blocks * tile
    width = panels * share
    rows = 2 * chips * share
    return pl.pallas_call(
        functools.partial(strip_kernel, panels, blocks, tile, chips),
        grid_spec=pltpu.PrefetchScalarGridSpec(
            num_scalar_prefetch=3,
            grid=(2 * chips,),
            in_specs=[
                pl.BlockSpec(
                    (share * panels, tile), lambda p, ids, live, cols: (block_of(ids, p, chips), 0)
                ),
            ],
            out_specs=[
                pl.BlockSpec((share, width), lambda p, ids, live, cols: (p, 0)),
                pl.BlockSpec((width, share), lambda p, ids, live, cols: (0, p)),
            ],
        ),
        out_shape=[
            jax.ShapeDtypeStruct((rows, width), BF16),
            jax.ShapeDtypeStruct((width, rows), BF16),
        ],
        compiler_params=params(),
        name="build_strip",
    )(ids, live, cols, masks)


def stack_features(ids_ref, feature_refs, held):
    share = feature_refs[0].shape[0]
    for k, ref in enumerate(feature_refs):
        at = pl.multiple_of((ids_ref[1] ^ k) * share, share)
        held[pl.ds(at, share), :] = ref[...]


def away_sums_kernel(n, start, ids_ref, dense_ref, *refs):
    out_ref, held_ref = refs[n:]
    stack_features(ids_ref, refs[:n], held_ref)
    rows = dense_ref[start : start + out_ref.shape[0], :]
    out_ref[...] = dot(rows, held_ref[...]).astype(BF16)


def away_far_sums(ids, dense, features, first):
    share, width = features[0].shape
    n = len(features)
    return pl.pallas_call(
        functools.partial(away_sums_kernel, n, first * share),
        in_specs=[pl.BlockSpec(memory_space=pltpu.SMEM)] + whole(1 + n),
        out_specs=whole(2),
        out_shape=[
            jax.ShapeDtypeStruct((share, width), BF16),
            jax.ShapeDtypeStruct((n * share, width), BF16),
        ],
        compiler_params=params(),
        name="away_far",
    )(ids, dense, *features)


def away_near_kernel(dense_ref, held_ref, *out_refs):
    share = out_refs[0].shape[0]
    total = dot(dense_ref[0 : len(out_refs) * share, :], held_ref[...])
    for q, ref in enumerate(out_refs):
        ref[...] = total[q * share : (q + 1) * share, :].astype(BF16)


def away_near_sums(dense, held, count, share):
    return pl.pallas_call(
        away_near_kernel,
        in_specs=whole(2),
        out_specs=whole(count),
        out_shape=[jax.ShapeDtypeStruct((share, held.shape[1]), BF16)] * count,
        compiler_params=params(),
        name="away_near",
    )(dense, held)


def chip_sums_kernel(start, dense_ref, held_ref, *refs):
    m = len(refs) // 2
    share = refs[0].shape[0]
    total = dot(dense_ref[start : start + m * share, :], held_ref[...])
    for q in range(m):
        part = total[q * share : (q + 1) * share, :] + refs[q][...].astype(F32)
        refs[m + q][...] = part.astype(refs[m + q].dtype)


def chip_sums(dense, received, held, first, dtypes, name):
    share, width = received[0].shape
    return pl.pallas_call(
        functools.partial(chip_sums_kernel, first * share),
        in_specs=whole(2 + len(received)),
        out_specs=whole(len(received)),
        out_shape=[jax.ShapeDtypeStruct((share, width), dtype) for dtype in dtypes],
        compiler_params=params(),
        name=name,
    )(dense, held, *received)


def add_far_kernel(own_ref, far_ref, out_ref):
    out_ref[...] = own_ref[...] + far_ref[...].astype(F32)


def add_far(own, far):
    return pl.pallas_call(
        add_far_kernel,
        in_specs=whole(2),
        out_specs=pl.BlockSpec(memory_space=pltpu.VMEM),
        out_shape=jax.ShapeDtypeStruct(own.shape, F32),
        cost_estimate=cost(10000000, 10**6),
        compiler_params=params(),
        name="add_far",
    )(own, far)


def rows_kernel(m, scale, ids_ref, own_ref, ws_ref, wn_ref, bias_ref, deg_ref, cot_ref, agg_ref, *refs):
    hidden_ref, dpre_ref, msg_ref, away_ref, keep_ref = refs[m - 1 :]
    width = own_ref.shape[1]
    agg = agg_ref[...]
    for ref in refs[: m - 1]:
        agg = agg + ref[...].astype(F32)
    deg = deg_ref[...]
    mean = (agg / deg).astype(BF16)
    v = dot(own_ref[...], ws_ref[...]) + dot(mean, wn_ref[...]) + bias_ref[...]
    t = jnp.tanh(GELU_A * (v + GELU_B * (v * v * v)))
    hidden_ref[...] = (0.5 * v * (1.0 + t)).astype(BF16)
    slope = 0.5 * (1.0 + t) + 0.5 * v * (1.0 - t * t) * (GELU_A * (1.0 + 3.0 * GELU_B * v * v))
    dpre = cot_ref[...].astype(F32) * slope
    dpre_b = dpre.astype(BF16)
    dpre_ref[...] = dpre_b
    msg_ref[...] = (dot(dpre_b, wn_ref[...], CONTRACT_SECOND) / deg).astype(BF16)
    dbias = jnp.broadcast_to(jnp.sum(dpre, axis=0, keepdims=True) * scale, (BIAS_ROWS, width))
    away_ref[width:, :] = dbias
    keep_ref[width:, :] = dbias
    first = (ids_ref[0] & 1) == 0
    mine = jnp.where(first, own_ref[...], mean)
    other = jnp.where(first, mean, own_ref[...])
    keep_ref[0:width, :] = dot(mine, dpre_b, CONTRACT_FIRST) * scale
    away_ref[0:width, :] = dot(other, dpre_b, CONTRACT_FIRST) * scale


def rows_step(ids, own, ws, wn, bias, deg, cot, agg, recvs, scale):
    share, width = own.shape
    block = jax.ShapeDtypeStruct((share, width), BF16)
    grads = jax.ShapeDtypeStruct((width + BIAS_ROWS, width), F32)
    m = len(recvs) + 1
    return pl.pallas_call(
        functools.partial(rows_kernel, m, scale),
        in_specs=[pl.BlockSpec(memory_space=pltpu.SMEM)] + whole(7 + m - 1),
        out_specs=whole(5),
        out_shape=[block, block, block, grads, grads],
        compiler_params=params(),
        name="rows_step",
    )(ids, own, ws, wn, bias, deg, cot, agg, *recvs)


def store_rounded(out_ref, total):
    rows = total.shape[0]
    tail = total[rows - BIAS_ROWS :, :]
    tail_high = tail.astype(BF16).astype(F32)
    index = lax.broadcasted_iota(jnp.int32, tail.shape, 0)
    mixed = jnp.where(index < BIAS_ROWS // 2, tail_high, tail - tail_high)
    out_ref[0 : rows - BIAS_ROWS, :] = total[0 : rows - BIAS_ROWS, :].astype(BF16)
    out_ref[rows - BIAS_ROWS :, :] = mixed.astype(BF16)


def load_sum(refs):
    rows = refs[0].shape[0]
    body = tree_sum(ref[0 : rows - BIAS_ROWS, :].astype(F32) for ref in refs)
    tail = tree_sum(ref[rows - BIAS_ROWS :, :].astype(F32) for ref in refs)
    return body, tail[0:1, :] + tail[BIAS_ROWS // 2 : BIAS_ROWS // 2 + 1, :]


def pair_grads_kernel(keep_ref, recv_ref, out_ref):
    store_rounded(out_ref, keep_ref[...] + recv_ref[...])


def pair_grads(keep, recv):
    return pl.pallas_call(
        pair_grads_kernel,
        in_specs=whole(2),
        out_specs=pl.BlockSpec(memory_space=pltpu.VMEM),
        out_shape=jax.ShapeDtypeStruct(keep.shape, BF16),
        compiler_params=params(),
        name="pair_grads",
    )(keep, recv)


def line_grads_kernel(n, *refs):
    body, line = load_sum(refs[:n])
    tail = jnp.broadcast_to(line, (BIAS_ROWS, line.shape[1]))
    store_rounded(refs[-1], jnp.concatenate([body, tail], axis=0))


def line_grads(parts):
    n = len(parts)
    return pl.pallas_call(
        functools.partial(line_grads_kernel, n),
        in_specs=whole(n),
        out_specs=pl.BlockSpec(memory_space=pltpu.VMEM),
        out_shape=jax.ShapeDtypeStruct(parts[0].shape, BF16),
        compiler_params=params(),
        name="line_grads",
    )(*parts)


def all_grads_kernel(n, *refs):
    body, line = load_sum(refs[:n])
    refs[n][...] = body
    refs[n + 1][...] = line


def all_grads(parts):
    n = len(parts)
    rows, width = parts[0].shape
    return pl.pallas_call(
        functools.partial(all_grads_kernel, n),
        in_specs=whole(n),
        out_specs=whole(2),
        out_shape=[
            jax.ShapeDtypeStruct((rows - BIAS_ROWS, width), F32),
            jax.ShapeDtypeStruct((1, width), F32),
        ],
        compiler_params=params(),
        name="all_grads",
    )(*parts)


def place_grads_kernel(ids_ref, mine_ref, other_ref, line_ref, after_ref, self_ref, neigh_ref, bias_ref):
    first = (ids_ref[0] & 1) == 0
    self_ref[...] = jnp.where(first, mine_ref[...], other_ref[...])
    neigh_ref[...] = jnp.where(first, other_ref[...], mine_ref[...])
    bias_ref[...] = line_ref[...]


def place_grads(ids, mine, other, line, after):
    out = jax.ShapeDtypeStruct(mine.shape, F32)
    return pl.pallas_call(
        place_grads_kernel,
        in_specs=[pl.BlockSpec(memory_space=pltpu.SMEM)]
        + whole(3)
        + [pl.BlockSpec(memory_space=pl.ANY)],
        out_specs=whole(3),
        out_shape=[out, out, jax.ShapeDtypeStruct(line.shape, F32)],
        compiler_params=params(),
        name="place_grads",
    )(ids, mine, other, line, after)


def extend_kernel(in_ref, out_ref):
    rows = in_ref.shape[0]
    out_ref[0:rows, :] = in_ref[...]
    out_ref[rows:, :] = jnp.zeros((out_ref.shape[0] - rows, out_ref.shape[1]), out_ref.dtype)


def extend(value):
    rows, width = value.shape
    return pl.pallas_call(
        extend_kernel,
        in_specs=whole(1),
        out_specs=pl.BlockSpec(memory_space=pltpu.VMEM),
        out_shape=jax.ShapeDtypeStruct((rows + FAR_ROWS, width), value.dtype),
        compiler_params=params(),
        name="extend",
    )(value)


def back_kernel(n, ids_ref, flip_ref, *refs):
    own_ref, out_refs, held, total = refs[n], refs[n + 1 : -2], refs[-2], refs[-1]
    share = own_ref.shape[0]
    for q, ref in enumerate(refs[:n]):
        held[q * share : (q + 1) * share, :] = ref[0:share, :]
    total[...] = dot(flip_ref[...], held[...])
    own_ref[...] = total[pl.ds(pl.multiple_of(ids_ref[1] * share, share), share), :]
    for k, ref in enumerate(out_refs):
        at = pl.multiple_of((ids_ref[1] ^ (k + 1)) * share, share)
        ref[...] = total[pl.ds(at, share), :].astype(BF16)


def back_sums(ids, flip, messages, panels):
    share, width = messages[0].shape
    n = len(messages)
    block = jax.ShapeDtypeStruct((share, width), BF16)
    return pl.pallas_call(
        functools.partial(back_kernel, n),
        in_specs=[pl.BlockSpec(memory_space=pltpu.SMEM)] + whole(1 + n),
        out_specs=whole(panels),
        out_shape=[jax.ShapeDtypeStruct((share, width), F32)] + [block] * (panels - 1),
        scratch_shapes=[
            pltpu.VMEM((n * share, width), BF16),
            pltpu.VMEM((panels * share, width), F32),
        ],
        compiler_params=params(),
        name="back_sums",
    )(ids, flip, *messages)


def feature_grads_kernel(n, dpre_ref, ws_ref, own_ref, *refs):
    total = own_ref[...]
    for ref in refs[:n]:
        total = total + ref[...].astype(F32)
    total = total + dot(dpre_ref[...], ws_ref[...], CONTRACT_SECOND)
    refs[n][...] = total.astype(BF16)
    refs[n + 1][...] = jnp.zeros_like(refs[n + 1])


def feature_grads(dpre, ws, own, recvs):
    return pl.pallas_call(
        functools.partial(feature_grads_kernel, len(recvs)),
        in_specs=whole(3 + len(recvs)),
        out_specs=whole(2),
        out_shape=[jax.ShapeDtypeStruct(dpre.shape, BF16), jax.ShapeDtypeStruct((SPACER_ROWS, dpre.shape[1]), BF16)],
        compiler_params=params(),
        name="feature_grads",
    )(dpre, ws, own, *recvs)


def per_device(
    features,
    self_weight,
    neigh_weight,
    out_bias,
    tile_masks,
    tile_live,
    tile_columns,
    node_degree,
    cotangent,
):
    row_devices = lax.axis_size("row")
    rep_devices = lax.axis_size("rep")
    chips = rep_devices // 2
    panel_rows, width = features.shape
    share = node_degree.shape[0]
    panels = tile_masks.shape[1]
    tile = tile_masks.shape[2]
    blocks = share // tile
    scale = 1.0 / math.sqrt(share * row_devices * rep_devices)
    rep, row = lax.axis_index("rep"), lax.axis_index("row")
    ids = jnp.stack([rep, row]).astype(jnp.int32)

    own = lax.dynamic_slice_in_dim(features, rep * share, share, 0)
    gathered = [own] + [xor_permute(own, "row", k) for k in range(1, row_devices)]
    dense, flip = build_strip(
        ids, tile_masks.reshape(panel_rows * panels, tile), tile_live.T, tile_columns.T,
        panels, blocks, tile, chips,
    )
    deg = jnp.broadcast_to(node_degree.astype(F32)[:, None], (share, width))

    last = chips - 1
    away_far, held = away_far_sums(ids, dense, gathered, last)
    away = away_near_sums(dense, held, last, share)
    (far,) = chip_sums(dense, [xor_permute(away_far, "rep", 1)], held, chips + last, [BF16], "chip_far")
    far = xor_permute(far, "rep", 2 * last)
    sums = chip_sums(
        dense, [xor_permute(value, "rep", 1) for value in away], held, chips,
        [F32] + [BF16] * (last - 1), "chip_near",
    )
    recvs = [xor_permute(sums[q], "rep", 2 * q) for q in reversed(range(1, last))]
    agg = add_far(sums[0], far)
    hidden_out, dpre, message, grad_away, grad_keep = rows_step(
        ids, own, self_weight, neigh_weight, out_bias[None, :], deg, cotangent, agg, recvs, scale
    )

    even = [xor_permute(message, "rep", 2 * q) for q in reversed(range(1, chips))]
    even = [message] + even[::-1]
    odd = [xor_permute(value, "rep", 1) for value in even[:last] + [extend(even[last])]]
    spread = back_sums(ids, flip, odd + even, panels)

    line = pair_grads(grad_keep, xor_permute(grad_away, "rep", 1))
    k = row_devices // 2
    while k:
        line = line_grads([line, xor_permute(line, "row", k)])
        k //= 2
    arrived = [xor_permute(spread[k], "row", k) for k in range(1, row_devices)]
    grad_features, spacer = feature_grads(dpre, self_weight, spread[0], arrived)
    late = xor_permute(spacer, "rep", 1)
    mine, bias_line = all_grads(
        [line] + [xor_permute(line, "rep", 2 * q) for q in range(1, chips)]
    )
    grad_self, grad_neigh, grad_bias = place_grads(
        ids, mine, xor_permute(mine, "rep", 1), bias_line, late
    )
    return (hidden_out, grad_features, grad_self, grad_neigh, grad_bias[0])


def solution(mesh):
    return jax.shard_map(
        per_device,
        mesh=mesh,
        in_specs=(
            P("row", None),
            P(),
            P(),
            P(),
            P("row", "rep", None),
            P("row", "rep"),
            P("row", "rep"),
            P(("row", "rep")),
            P(("row", "rep"), None),
        ),
        out_specs=(P(("row", "rep"), None), P(("row", "rep"), None), P(), P(), P()),
        check_vma=False,
    )
```

```python
import functools
import math

import jax
import jax.numpy as jnp
from jax import lax
from jax.experimental import pallas as pl
from jax.experimental.pallas import tpu as pltpu
from jax.sharding import PartitionSpec as P

BF16 = jnp.bfloat16
F32 = jnp.float32
BIAS_ROWS = 16
SPACER_ROWS = 304
FAR_ROWS = 32
VMEM_LIMIT = 40 * 1024 * 1024
CONTRACT_FIRST = (((0,), (0,)), ((), ()))
CONTRACT_SECOND = (((1,), (1,)), ((), ()))
GELU_A = math.sqrt(2.0 / math.pi)
GELU_B = 0.044715


def dot(a, b, dims=(((1,), (0,)), ((), ()))):
    return lax.dot_general(a, b, dims, preferred_element_type=F32)


def params():
    return pltpu.CompilerParams(vmem_limit_bytes=VMEM_LIMIT)


def cost(flops, bytes_accessed):
    return pl.CostEstimate(flops=flops, bytes_accessed=bytes_accessed, transcendentals=0)


def whole(n):
    return [pl.BlockSpec(memory_space=pltpu.VMEM)] * n


def tree_sum(terms):
    terms = list(terms)
    while len(terms) > 1:
        terms = [a + b for a, b in zip(terms[::2], terms[1::2])]
    return terms[0]


def xor_permute(value, axis, k):
    return lax.ppermute(value, axis, [(i, i ^ k) for i in range(lax.axis_size(axis))])


def block_of(ids, p, chips):
    return (ids[0] ^ (1 - p // chips)) ^ (2 * (p % chips))


def strip_kernel(panels, blocks, tile, chips, ids_ref, live_ref, cols_ref, mask_ref, dense_ref, flip_ref):
    step = block_of(ids_ref, pl.program_id(0), chips)
    for j in range(blocks):
        i = step * blocks + j
        for s in range(panels):
            bits = mask_ref[pl.ds(j * tile * panels + s, tile, stride=panels), :].astype(F32)
            turned = bits.T
            live = live_ref[s, i] != 0
            col = cols_ref[s, i]
            for b in range(blocks):
                keep = jnp.where(live & (col == b), 1.0, 0.0).astype(F32)
                at = (s * blocks + b) * tile
                dense_ref[j * tile : (j + 1) * tile, at : at + tile] = (bits * keep).astype(BF16)
                flip_ref[at : at + tile, j * tile : (j + 1) * tile] = (turned * keep).astype(BF16)


def build_strip(ids, masks, live, cols, panels, blocks, tile, chips):
    share = blocks * tile
    width = panels * share
    rows = 2 * chips * share
    return pl.pallas_call(
        functools.partial(strip_kernel, panels, blocks, tile, chips),
        grid_spec=pltpu.PrefetchScalarGridSpec(
            num_scalar_prefetch=3,
            grid=(2 * chips,),
            in_specs=[
                pl.BlockSpec(
                    (share * panels, tile), lambda p, ids, live, cols: (block_of(ids, p, chips), 0)
                ),
            ],
            out_specs=[
                pl.BlockSpec((share, width), lambda p, ids, live, cols: (p, 0)),
                pl.BlockSpec((width, share), lambda p, ids, live, cols: (0, p)),
            ],
        ),
        out_shape=[
            jax.ShapeDtypeStruct((rows, width), BF16),
            jax.ShapeDtypeStruct((width, rows), BF16),
        ],
        compiler_params=params(),
        name="build_strip",
    )(ids, live, cols, masks)


def stack_features(ids_ref, feature_refs, held):
    share = feature_refs[0].shape[0]
    for k, ref in enumerate(feature_refs):
        at = pl.multiple_of((ids_ref[1] ^ k) * share, share)
        held[pl.ds(at, share), :] = ref[...]


def away_sums_kernel(n, start, ids_ref, dense_ref, *refs):
    out_ref, held_ref = refs[n:]
    stack_features(ids_ref, refs[:n], held_ref)
    rows = dense_ref[start : start + out_ref.shape[0], :]
    out_ref[...] = dot(rows, held_ref[...]).astype(BF16)


def away_far_sums(ids, dense, features, first):
    share, width = features[0].shape
    n = len(features)
    return pl.pallas_call(
        functools.partial(away_sums_kernel, n, first * share),
        in_specs=[pl.BlockSpec(memory_space=pltpu.SMEM)] + whole(1 + n),
        out_specs=whole(2),
        out_shape=[
            jax.ShapeDtypeStruct((share, width), BF16),
            jax.ShapeDtypeStruct((n * share, width), BF16),
        ],
        compiler_params=params(),
        name="away_far",
    )(ids, dense, *features)


def away_near_kernel(dense_ref, held_ref, *out_refs):
    share = out_refs[0].shape[0]
    total = dot(dense_ref[0 : len(out_refs) * share, :], held_ref[...])
    for q, ref in enumerate(out_refs):
        ref[...] = total[q * share : (q + 1) * share, :].astype(BF16)


def away_near_sums(dense, held, count, share):
    return pl.pallas_call(
        away_near_kernel,
        in_specs=whole(2),
        out_specs=whole(count),
        out_shape=[jax.ShapeDtypeStruct((share, held.shape[1]), BF16)] * count,
        compiler_params=params(),
        name="away_near",
    )(dense, held)


def chip_sums_kernel(start, dense_ref, held_ref, *refs):
    m = len(refs) // 2
    share = refs[0].shape[0]
    total = dot(dense_ref[start : start + m * share, :], held_ref[...])
    for q in range(m):
        part = total[q * share : (q + 1) * share, :] + refs[q][...].astype(F32)
        refs[m + q][...] = part.astype(refs[m + q].dtype)


def chip_sums(dense, received, held, first, dtypes, name):
    share, width = received[0].shape
    return pl.pallas_call(
        functools.partial(chip_sums_kernel, first * share),
        in_specs=whole(2 + len(received)),
        out_specs=whole(len(received)),
        out_shape=[jax.ShapeDtypeStruct((share, width), dtype) for dtype in dtypes],
        compiler_params=params(),
        name=name,
    )(dense, held, *received)


def add_far_kernel(own_ref, far_ref, out_ref):
    out_ref[...] = own_ref[...] + far_ref[...].astype(F32)


def add_far(own, far):
    return pl.pallas_call(
        add_far_kernel,
        in_specs=whole(2),
        out_specs=pl.BlockSpec(memory_space=pltpu.VMEM),
        out_shape=jax.ShapeDtypeStruct(own.shape, F32),
        cost_estimate=cost(10000000, 10**6),
        compiler_params=params(),
        name="add_far",
    )(own, far)


def rows_kernel(m, scale, ids_ref, own_ref, ws_ref, wn_ref, bias_ref, deg_ref, cot_ref, agg_ref, *refs):
    hidden_ref, dpre_ref, msg_ref, away_ref, keep_ref = refs[m - 1 :]
    width = own_ref.shape[1]
    agg = agg_ref[...]
    for ref in refs[: m - 1]:
        agg = agg + ref[...].astype(F32)
    deg = deg_ref[...]
    mean = (agg / deg).astype(BF16)
    v = dot(own_ref[...], ws_ref[...]) + dot(mean, wn_ref[...]) + bias_ref[...]
    t = jnp.tanh(GELU_A * (v + GELU_B * (v * v * v)))
    hidden_ref[...] = (0.5 * v * (1.0 + t)).astype(BF16)
    slope = 0.5 * (1.0 + t) + 0.5 * v * (1.0 - t * t) * (GELU_A * (1.0 + 3.0 * GELU_B * v * v))
    dpre = cot_ref[...].astype(F32) * slope
    dpre_b = dpre.astype(BF16)
    dpre_ref[...] = dpre_b
    msg_ref[...] = (dot(dpre_b, wn_ref[...], CONTRACT_SECOND) / deg).astype(BF16)
    dbias = jnp.broadcast_to(jnp.sum(dpre, axis=0, keepdims=True) * scale, (BIAS_ROWS, width))
    away_ref[width:, :] = dbias
    keep_ref[width:, :] = dbias
    first = (ids_ref[0] & 1) == 0
    mine = jnp.where(first, own_ref[...], mean)
    other = jnp.where(first, mean, own_ref[...])
    keep_ref[0:width, :] = dot(mine, dpre_b, CONTRACT_FIRST) * scale
    away_ref[0:width, :] = dot(other, dpre_b, CONTRACT_FIRST) * scale


def rows_step(ids, own, ws, wn, bias, deg, cot, agg, recvs, scale):
    share, width = own.shape
    block = jax.ShapeDtypeStruct((share, width), BF16)
    grads = jax.ShapeDtypeStruct((width + BIAS_ROWS, width), F32)
    m = len(recvs) + 1
    return pl.pallas_call(
        functools.partial(rows_kernel, m, scale),
        in_specs=[pl.BlockSpec(memory_space=pltpu.SMEM)] + whole(7 + m - 1),
        out_specs=whole(5),
        out_shape=[block, block, block, grads, grads],
        compiler_params=params(),
        name="rows_step",
    )(ids, own, ws, wn, bias, deg, cot, agg, *recvs)


def store_rounded(out_ref, total):
    rows = total.shape[0]
    tail = total[rows - BIAS_ROWS :, :]
    tail_high = tail.astype(BF16).astype(F32)
    index = lax.broadcasted_iota(jnp.int32, tail.shape, 0)
    mixed = jnp.where(index < BIAS_ROWS // 2, tail_high, tail - tail_high)
    out_ref[0 : rows - BIAS_ROWS, :] = total[0 : rows - BIAS_ROWS, :].astype(BF16)
    out_ref[rows - BIAS_ROWS :, :] = mixed.astype(BF16)


def load_sum(refs):
    rows = refs[0].shape[0]
    body = tree_sum(ref[0 : rows - BIAS_ROWS, :].astype(F32) for ref in refs)
    tail = tree_sum(ref[rows - BIAS_ROWS :, :].astype(F32) for ref in refs)
    return body, tail[0:1, :] + tail[BIAS_ROWS // 2 : BIAS_ROWS // 2 + 1, :]


def pair_grads_kernel(keep_ref, recv_ref, out_ref):
    store_rounded(out_ref, keep_ref[...] + recv_ref[...])


def pair_grads(keep, recv):
    return pl.pallas_call(
        pair_grads_kernel,
        in_specs=whole(2),
        out_specs=pl.BlockSpec(memory_space=pltpu.VMEM),
        out_shape=jax.ShapeDtypeStruct(keep.shape, BF16),
        compiler_params=params(),
        name="pair_grads",
    )(keep, recv)


def line_grads_kernel(n, *refs):
    body, line = load_sum(refs[:n])
    tail = jnp.broadcast_to(line, (BIAS_ROWS, line.shape[1]))
    store_rounded(refs[-1], jnp.concatenate([body, tail], axis=0))


def line_grads(parts):
    n = len(parts)
    return pl.pallas_call(
        functools.partial(line_grads_kernel, n),
        in_specs=whole(n),
        out_specs=pl.BlockSpec(memory_space=pltpu.VMEM),
        out_shape=jax.ShapeDtypeStruct(parts[0].shape, BF16),
        compiler_params=params(),
        name="line_grads",
    )(*parts)


def all_grads_kernel(n, *refs):
    body, line = load_sum(refs[:n])
    half = body.shape[0] // 2
    refs[n][...] = body[:half, :]
    refs[n + 1][...] = body[half:, :]
    refs[n + 2][...] = line


def all_grads(parts):
    n = len(parts)
    rows, width = parts[0].shape
    half = jax.ShapeDtypeStruct(((rows - BIAS_ROWS) // 2, width), F32)
    return pl.pallas_call(
        functools.partial(all_grads_kernel, n),
        in_specs=whole(n),
        out_specs=whole(3),
        out_shape=[half, half, jax.ShapeDtypeStruct((1, width), F32)],
        compiler_params=params(),
        name="all_grads",
    )(*parts)


def place_grads_kernel(ids_ref, *refs):
    mine_refs, other_refs, (line_ref, after_ref, self_ref, neigh_ref, bias_ref) = refs[:2], refs[2:4], refs[4:]
    first = (ids_ref[0] & 1) == 0
    half = refs[0].shape[0]
    for k, (mine_ref, other_ref) in enumerate(zip(mine_refs, other_refs)):
        at = slice(k * half, (k + 1) * half)
        self_ref[at, :] = jnp.where(first, mine_ref[...], other_ref[...])
        neigh_ref[at, :] = jnp.where(first, other_ref[...], mine_ref[...])
    bias_ref[...] = line_ref[...]


def place_grads(ids, mine, other, line, after):
    rows, width = mine[0].shape
    out = jax.ShapeDtypeStruct((2 * rows, width), F32)
    return pl.pallas_call(
        place_grads_kernel,
        in_specs=[pl.BlockSpec(memory_space=pltpu.SMEM)]
        + whole(5)
        + [pl.BlockSpec(memory_space=pl.ANY)],
        out_specs=whole(3),
        out_shape=[out, out, jax.ShapeDtypeStruct(line.shape, F32)],
        compiler_params=params(),
        name="place_grads",
    )(ids, *mine, *other, line, after)


def extend_kernel(in_ref, out_ref):
    rows = in_ref.shape[0]
    out_ref[0:rows, :] = in_ref[...]
    out_ref[rows:, :] = jnp.zeros((out_ref.shape[0] - rows, out_ref.shape[1]), out_ref.dtype)


def extend(value):
    rows, width = value.shape
    return pl.pallas_call(
        extend_kernel,
        in_specs=whole(1),
        out_specs=pl.BlockSpec(memory_space=pltpu.VMEM),
        out_shape=jax.ShapeDtypeStruct((rows + FAR_ROWS, width), value.dtype),
        compiler_params=params(),
        name="extend",
    )(value)


def back_kernel(n, ids_ref, flip_ref, *refs):
    own_ref, out_refs, held, total = refs[n], refs[n + 1 : -2], refs[-2], refs[-1]
    share = own_ref.shape[0]
    for q, ref in enumerate(refs[:n]):
        held[q * share : (q + 1) * share, :] = ref[0:share, :]
    total[...] = dot(flip_ref[...], held[...])
    own_ref[...] = total[pl.ds(pl.multiple_of(ids_ref[1] * share, share), share), :]
    for k, ref in enumerate(out_refs):
        at = pl.multiple_of((ids_ref[1] ^ (k + 1)) * share, share)
        ref[...] = total[pl.ds(at, share), :].astype(BF16)


def back_sums(ids, flip, messages, panels):
    share, width = messages[0].shape
    n = len(messages)
    block = jax.ShapeDtypeStruct((share, width), BF16)
    return pl.pallas_call(
        functools.partial(back_kernel, n),
        in_specs=[pl.BlockSpec(memory_space=pltpu.SMEM)] + whole(1 + n),
        out_specs=whole(panels),
        out_shape=[jax.ShapeDtypeStruct((share, width), F32)] + [block] * (panels - 1),
        scratch_shapes=[
            pltpu.VMEM((n * share, width), BF16),
            pltpu.VMEM((panels * share, width), F32),
        ],
        compiler_params=params(),
        name="back_sums",
    )(ids, flip, *messages)


def feature_grads_kernel(n, dpre_ref, ws_ref, own_ref, *refs):
    total = own_ref[...]
    for ref in refs[:n]:
        total = total + ref[...].astype(F32)
    total = total + dot(dpre_ref[...], ws_ref[...], CONTRACT_SECOND)
    refs[n][...] = total.astype(BF16)
    refs[n + 1][...] = jnp.zeros_like(refs[n + 1])


def feature_grads(dpre, ws, own, recvs):
    return pl.pallas_call(
        functools.partial(feature_grads_kernel, len(recvs)),
        in_specs=whole(3 + len(recvs)),
        out_specs=whole(2),
        out_shape=[jax.ShapeDtypeStruct(dpre.shape, BF16), jax.ShapeDtypeStruct((SPACER_ROWS, dpre.shape[1]), BF16)],
        compiler_params=params(),
        name="feature_grads",
    )(dpre, ws, own, *recvs)


def per_device(
    features,
    self_weight,
    neigh_weight,
    out_bias,
    tile_masks,
    tile_live,
    tile_columns,
    node_degree,
    cotangent,
):
    row_devices = lax.axis_size("row")
    rep_devices = lax.axis_size("rep")
    chips = rep_devices // 2
    panel_rows, width = features.shape
    share = node_degree.shape[0]
    panels = tile_masks.shape[1]
    tile = tile_masks.shape[2]
    blocks = share // tile
    scale = 1.0 / math.sqrt(share * row_devices * rep_devices)
    rep, row = lax.axis_index("rep"), lax.axis_index("row")
    ids = jnp.stack([rep, row]).astype(jnp.int32)

    own = lax.dynamic_slice_in_dim(features, rep * share, share, 0)
    gathered = [own] + [xor_permute(own, "row", k) for k in range(1, row_devices)]
    dense, flip = build_strip(
        ids, tile_masks.reshape(panel_rows * panels, tile), tile_live.T, tile_columns.T,
        panels, blocks, tile, chips,
    )
    deg = jnp.broadcast_to(node_degree.astype(F32)[:, None], (share, width))

    last = chips - 1
    away_far, held = away_far_sums(ids, dense, gathered, last)
    away = away_near_sums(dense, held, last, share)
    (far,) = chip_sums(dense, [xor_permute(away_far, "rep", 1)], held, chips + last, [BF16], "chip_far")
    far = xor_permute(far, "rep", 2 * last)
    sums = chip_sums(
        dense, [xor_permute(value, "rep", 1) for value in away], held, chips,
        [F32] + [BF16] * (last - 1), "chip_near",
    )
    recvs = [xor_permute(sums[q], "rep", 2 * q) for q in reversed(range(1, last))]
    agg = add_far(sums[0], far)
    hidden_out, dpre, message, grad_away, grad_keep = rows_step(
        ids, own, self_weight, neigh_weight, out_bias[None, :], deg, cotangent, agg, recvs, scale
    )

    even = [xor_permute(message, "rep", 2 * q) for q in reversed(range(1, chips))]
    even = [message] + even[::-1]
    odd = [xor_permute(value, "rep", 1) for value in even[:last] + [extend(even[last])]]
    spread = back_sums(ids, flip, odd + even, panels)

    line = pair_grads(grad_keep, xor_permute(grad_away, "rep", 1))
    k = row_devices // 2
    while k:
        line = line_grads([line, xor_permute(line, "row", k)])
        k //= 2
    arrived = [xor_permute(spread[k], "row", k) for k in range(1, row_devices)]
    grad_features, spacer = feature_grads(dpre, self_weight, spread[0], arrived)
    late = xor_permute(spacer, "rep", 1)
    *mine, bias_line = all_grads(
        [line] + [xor_permute(line, "rep", 2 * q) for q in range(1, chips)]
    )
    other = [xor_permute(value, "rep", 1) for value in mine]
    grad_self, grad_neigh, grad_bias = place_grads(ids, mine, other, bias_line, late)
    return (hidden_out, grad_features, grad_self, grad_neigh, grad_bias[0])


def solution(mesh):
    return jax.shard_map(
        per_device,
        mesh=mesh,
        in_specs=(
            P("row", None),
            P(),
            P(),
            P(),
            P("row", "rep", None),
            P("row", "rep"),
            P("row", "rep"),
            P(("row", "rep")),
            P(("row", "rep"), None),
        ),
        out_specs=(P(("row", "rep"), None), P(("row", "rep"), None), P(), P(), P()),
        check_vma=False,
    )
```
